256 devices in a mesh: group: 8 (over y, core), tile: 32 (over x, z).
Axes of the slice: x: 4, y: 4, z: 8, core: 2. Of those that a mesh axis runs over, the one named last changes fastest.
Arguments:
- raw_pulses: bfloat16 [512, 4, 2, 16384], P(('group', 'tile')), may hold values from -6 to 6
- chirp_taps: float32 [2, 1024], replicated, may hold values from -0.125 to 0.125
- phase_error: float32 [512], P(('group', 'tile')), may hold values from -3.140625 to 3.140625
- illumination: int32 [256, 256, 2], P(('group', 'tile')), may hold values from 0 to 2, as said below
- swath_start: int32 [256, 256, 2], P(('group', 'tile')), may hold values from 0 to 124
- range_bins: int32 [256, 8, 256], P(('group', 'tile')), may hold values from 0 to 511
- cross_range: float32 [256, 256], P(('group', 'tile')), may hold values from -2 to 2
Outputs:
- image_tile: float32 [256, 4, 2, 256], P(('group', 'tile'))
- phase_grad: float32 [512], P(('group', 'tile'))
The draws below stay inside these ranges and needn't reach their ends.
Inputs may be any that keep to these rules, and one draw needn't show every extreme that they name: `illumination`: the local pulse of block d sent in slot c to tile e; 2 marks an empty slot; each tile has its own share of filled slots.
All inputs are finite; a program needn't handle non-finite values.
Results may differ from the reference program's by a relative error of at most 0.008.
Values may be sent and summed in bfloat16 or wider, within the bound.
No kernel may reach another device: no remote copies, remote signals or barrier semaphores. Data moves between devices by JAX's collectives and lax.ppermute only.
A program may use at most 128 MiB of HBM per device.

```python
import math
import jax
import jax.numpy as jnp
from jax import lax

RBINS = 16384
POLS = 4
TAPS = 1024
SWATH = 512
RSTEP = 128
CAP = 2
PULSE_DEV = 2
PIX = 256
GROUPS = 8
TILES_GROUP = 32
TILES = 256
PULSES = 512


def draw_illumination(key, part):
    key = jax.random.fold_in(key, 11)
    key_level, key_roll, key_pulse = jax.random.split(key, 3)
    level = jax.random.randint(key_level, (1, TILES, 1), 1, 9)
    roll_draw = jax.random.randint(key_roll, (TILES, TILES, CAP), 0, 8)
    pulse_draw = jax.random.randint(key_pulse, (TILES, TILES, CAP), 0, PULSE_DEV)
    return jnp.where(roll_draw < level, pulse_draw, PULSE_DEV).astype(jnp.int32)


def place_ends(drawn, rng, least, largest):
    longest = drawn.shape.index(max(drawn.shape))
    spots = []
    for shift in (0, 1):
        where = [jax.random.randint(jax.random.fold_in(rng, axis), (), 0, length) for axis, length in enumerate(drawn.shape)]
        where[longest] = (where[longest] + shift) % drawn.shape[longest]
        spots.append(tuple(where))
    return drawn.at[spots[0]].set(least).at[spots[1]].set(largest)


def block_levels(key, dims, pieces, low, largest):
    level = 1.0
    for position, parts in pieces:
        steps = jax.random.uniform(jax.random.fold_in(jax.random.fold_in(key, 6), position), (parts,), jnp.float32, low / len(pieces), largest / len(pieces))
        level = level * jnp.repeat(jnp.exp(steps), dims[position] // parts).reshape((-1,) + (1,) * (len(dims) - 1 - position))
    return level


def noise(rng, extent, spread, most, cuts=(), kind=jnp.bfloat16):
    drawn = spread * jax.random.normal(rng, extent, jnp.float32)
    if cuts:
        drawn = drawn * block_levels(rng, extent, cuts, -0.22, 0.18)
    return jnp.clip(drawn, -most, most).astype(kind)


def setup_inputs(seed: int = 0) -> dict:
    key_list = jax.random.split(jax.random.key(seed), 8)
    return {
        "raw_pulses": noise(key_list[0], (PULSES, POLS, 2, RBINS), 1.0, 6.0, ((0, 256),)),
        "chirp_taps": noise(key_list[1], (2, TAPS), (2 * TAPS) ** -0.5, 0.125, (), jnp.float32),
        "phase_error": jnp.clip(jax.random.uniform(key_list[2], (PULSES,), jnp.float32, -3.140625, 3.140625), -3.140625, 3.140625),
        "illumination": draw_illumination(jax.random.fold_in(key_list[7], 71), 0),
        "swath_start": place_ends(jax.random.randint(key_list[4], (TILES, TILES, CAP), 0, (RBINS - SWATH) // RSTEP + 1), jax.random.fold_in(key_list[4], 1), 0, ((RBINS - SWATH) // RSTEP + 1) - 1).astype(jnp.int32),
        "range_bins": place_ends(jax.random.randint(key_list[5], (TILES, GROUPS, PIX), 0, SWATH), jax.random.fold_in(key_list[5], 1), 0, SWATH - 1).astype(jnp.int32),
        "cross_range": jnp.clip(jax.random.uniform(key_list[6], (TILES, PIX), jnp.float32, -2.0, 2.0) * block_levels(key_list[6], (TILES, PIX), ((0, 256),), -0.4, 0.0), -2.0, 2.0),
    }


def kappa_phase(bin_number):
    return (31 * bin_number % 97).astype(jnp.float32) * (2.0 * math.pi / 97.0)

def compress_pulses(raw_pulses, chirp_taps):
    rounded_taps = chirp_taps.astype(jnp.bfloat16).astype(jnp.float32)
    taps_spectrum = jnp.conj(jnp.fft.fft(lax.complex(rounded_taps[0], rounded_taps[1]), n=2 * RBINS))

    def filter_one(pulse_data):
        samples = pulse_data.astype(jnp.float32)
        signal = lax.complex(samples[:, 0], samples[:, 1])
        filtered = jnp.fft.ifft(jnp.fft.fft(signal, n=2 * RBINS, axis=-1) * taps_spectrum[None, :], axis=-1)[:, :RBINS]
        return jnp.stack([jnp.real(filtered), jnp.imag(filtered)], axis=1).astype(jnp.bfloat16)
    return lax.map(filter_one, raw_pulses)

def reference(raw_pulses, chirp_taps, phase_error, illumination, swath_start, range_bins, cross_range):
    compressed = compress_pulses(raw_pulses, chirp_taps)
    device_ids = jnp.arange(TILES, dtype=jnp.int32)
    look_rate = math.pi * (2 * device_ids + 1 - TILES).astype(jnp.float32) / TILES
    image_scale = 1.0 / math.sqrt(TILES * CAP)
    grad_scale = image_scale / math.sqrt(PIX * POLS)

    def take_swath(global_pulse, offset):
        zero = jnp.zeros((), jnp.int32)
        return lax.dynamic_slice(compressed, (global_pulse.astype(jnp.int32), zero, zero, offset.astype(jnp.int32)), (1, POLS, 2, SWATH))[0]

    def one_tile(target):
        chosen = lax.dynamic_index_in_dim(illumination, target, 1, keepdims=False)
        swath_offset = (RSTEP * lax.dynamic_index_in_dim(swath_start, target, 1, keepdims=False)).astype(jnp.int32)
        active = chosen < PULSE_DEV
        clamped = jnp.minimum(chosen, PULSE_DEV - 1)
        global_pulse = (device_ids[:, None] * PULSE_DEV + clamped).astype(jnp.int32)
        rotation = kappa_phase(swath_offset) - phase_error[global_pulse]
        cos_rot = jnp.where(active, jnp.cos(rotation), 0.0)[:, :, None, None]
        sin_rot = jnp.where(active, jnp.sin(rotation), 0.0)[:, :, None, None]
        swaths = jax.vmap(jax.vmap(take_swath))(global_pulse, swath_offset).astype(jnp.float32)
        real_part = cos_rot * swaths[:, :, :, 0] - sin_rot * swaths[:, :, :, 1]
        imag_part = sin_rot * swaths[:, :, :, 0] + cos_rot * swaths[:, :, :, 1]
        rotated = jnp.stack([real_part, imag_part], axis=3).astype(jnp.bfloat16)
        rotated = lax.optimization_barrier(rotated).astype(jnp.float32)
        bin_index = lax.dynamic_index_in_dim(range_bins, target, 0, keepdims=False)
        source_bins = jnp.repeat(bin_index, TILES_GROUP, axis=0)
        index_full = jnp.broadcast_to(source_bins[:, None, None, None, :], (TILES, CAP, POLS, 2, PIX))
        values = jnp.take_along_axis(rotated, index_full, axis=4)
        cross_row = lax.dynamic_index_in_dim(cross_range, target, 0, keepdims=False)
        phase_angle = kappa_phase(source_bins) + look_rate[:, None] * cross_row[None, :]
        cos_angle = jnp.cos(phase_angle)[:, None, None, :]
        sin_angle = jnp.sin(phase_angle)[:, None, None, :]
        values_real = values[:, :, :, 0]
        values_imag = values[:, :, :, 1]
        image_real = image_scale * lax.optimization_barrier(jnp.sum(cos_angle * values_real - sin_angle * values_imag, axis=(0, 1)))
        image_imag = image_scale * lax.optimization_barrier(jnp.sum(cos_angle * values_imag + sin_angle * values_real, axis=(0, 1)))
        magnitude = image_real * image_real + image_imag * image_imag
        grad_real = (4.0 * magnitude * image_real)[None, None]
        grad_imag = (-4.0 * magnitude * image_imag)[None, None]
        weighted_real = grad_real * cos_angle - grad_imag * sin_angle
        weighted_imag = grad_real * sin_angle + grad_imag * cos_angle
        slot_grad = grad_scale * lax.optimization_barrier(jnp.sum(weighted_real * values_imag + weighted_imag * values_real, axis=(2, 3)))
        return (jnp.stack([image_real, image_imag], axis=1), slot_grad)
    image_tile, slot_grads = lax.map(one_tile, jnp.arange(TILES, dtype=jnp.int32))
    pulse_ids = jnp.where(illumination < PULSE_DEV, device_ids[:, None, None] * PULSE_DEV + illumination, PULSES).astype(jnp.int32)
    contrib = jnp.transpose(slot_grads, (1, 0, 2))
    phase_grad = jax.ops.segment_sum(contrib.reshape(-1), pulse_ids.reshape(-1), num_segments=PULSES + 1)[:PULSES]
    return (image_tile, phase_grad)
```

```python
import functools
import math

import jax
import jax.numpy as jnp
from jax import lax
from jax.experimental import pallas as pl
from jax.experimental.pallas import tpu as pltpu
from jax.sharding import Mesh, PartitionSpec as P

TAPS = 1024
RBINS = 16384
POLS = 4
SWATH = 512
PIX = 256
TILES = 256
GROUPS = 8
PLANE = 32
ROWS = 2 * POLS
BLOCK = 256
BLOCKS = RBINS // BLOCK
NOTE_ROWS = 16
SPAN = TAPS + BLOCK
IMAGE_SCALE = 1.0 / math.sqrt(TILES * 2)
GRAD_SCALE = IMAGE_SCALE / math.sqrt(PIX * POLS)
VMEM_LIMIT = 48 * 1024 * 1024
BLOCK_ORDER = ((0, 0), (0, 1), (1, 0), (1, 1), (3, 0), (3, 1), (2, 0), (2, 1))
SMEM = pl.BlockSpec(memory_space=pltpu.SMEM)
VMEM = pl.BlockSpec(memory_space=pltpu.VMEM)
PARAMS = pltpu.CompilerParams(vmem_limit_bytes=VMEM_LIMIT)


def row_sign(shape, axis):
    return jnp.where(lax.broadcasted_iota(jnp.int32, shape, axis) < POLS, -1.0, 1.0)


def three_parts(x):
    first = x.astype(jnp.bfloat16).astype(jnp.float32)
    second = (x - first).astype(jnp.bfloat16).astype(jnp.float32)
    return [first, second, x - first - second]


def compress_kernel(
    raw_ref, taps_ref, error_ref, chosen_ref, start_ref, bins_ref, cross_ref, out_ref, known_ref, left_ref, odd_ref
):
    known = [bins_ref[...].astype(jnp.float32) - 256.0] + three_parts(cross_ref[...])
    known.append(jnp.zeros((5, PIX), jnp.float32))
    known = jnp.concatenate(known, axis=0).astype(jnp.bfloat16)
    for at in range(PLANE):
        known_ref[at] = known

    taps = taps_ref[...].astype(jnp.bfloat16).astype(jnp.float32)
    wide = []
    for part in range(2):
        rows = jnp.broadcast_to(taps[part : part + 1], (BLOCK, SPAN))
        wide.append(pltpu.roll(rows, 0, 1, stride=1, stride_axis=0))
    matrices = []
    for j in range(SPAN // BLOCK):
        lanes = slice(j * BLOCK, (j + 1) * BLOCK)
        matrices.append(jnp.concatenate([rows[:, lanes].T for rows in wide], axis=0).astype(jnp.bfloat16))

    total = BLOCKS * ROWS
    for pulse in range(2):
        first = raw_ref[pulse * total : (pulse + 1) * total].astype(jnp.float32)
        second = pltpu.roll(first.reshape(BLOCKS, ROWS, BLOCK), POLS, 1)
        second = (second * -row_sign((BLOCKS, ROWS, BLOCK), 1)).reshape(total, BLOCK)
        both = jnp.concatenate([first, second], axis=1)
        edge = jnp.zeros((SPAN // BLOCK * ROWS, 2 * BLOCK), jnp.float32)
        left_ref[...] = jnp.concatenate([both, edge[ROWS:]], axis=0).astype(jnp.bfloat16)
        odd_ref[...] = jnp.concatenate([both[ROWS:], edge], axis=0).astype(jnp.bfloat16)
        sums = None
        for j in range(SPAN // BLOCK):
            source = odd_ref if j % 2 else left_ref
            at = j // 2 * 2 * ROWS
            part = jnp.dot(source[at : at + total], matrices[j], preferred_element_type=jnp.float32)
            sums = part if sums is None else sums + part
        sums = sums.reshape(BLOCKS, ROWS, BLOCK)
        out_ref[pulse * BLOCKS : (pulse + 1) * BLOCKS] = jnp.concatenate(
            [sums[:, :, :128], sums[:, :, 128:]], axis=1
        ).astype(jnp.bfloat16)

    rows = [chosen_ref[...].astype(jnp.float32), start_ref[...].astype(jnp.float32)]
    for pulse in range(2):
        rows += three_parts(jnp.full((1, PIX), error_ref[pulse], jnp.float32))
    rows.append(jnp.zeros((NOTE_ROWS - 10, PIX), jnp.float32))
    rows = jnp.concatenate(rows, axis=0).astype(jnp.bfloat16)
    out_ref[2 * BLOCKS] = rows[:, :128]
    out_ref[2 * BLOCKS + 1] = rows[:, 128:]


def compress(raw, taps, phase_error, chosen, start, bins, cross):
    return pl.pallas_call(
        compress_kernel,
        out_shape=(
            jax.ShapeDtypeStruct((2 * BLOCKS + 2, 2 * ROWS, 128), jnp.bfloat16),
            jax.ShapeDtypeStruct((PLANE, 16, PIX), jnp.bfloat16),
        ),
        in_specs=[VMEM, VMEM, SMEM, VMEM, VMEM, VMEM, VMEM],
        out_specs=(VMEM, VMEM),
        scratch_shapes=[
            pltpu.VMEM((BLOCKS * ROWS + 4 * ROWS, 2 * BLOCK), jnp.bfloat16),
            pltpu.VMEM((BLOCKS * ROWS + 4 * ROWS, 2 * BLOCK), jnp.bfloat16),
        ],
        compiler_params=PARAMS,
        name="compress",
    )(raw, taps, phase_error, chosen, start, bins, cross)


def shift_kernel(count, *refs):
    out_ref = refs[count]
    for dev in range(count):
        out_ref[dev, 0] = refs[dev][: 2 * BLOCKS]
        rows = refs[dev][: 2 * BLOCKS].astype(jnp.float32)
        later = jnp.concatenate([rows[1:, :ROWS], rows[:1, :ROWS]], axis=0)
        out_ref[dev, 1] = jnp.concatenate([rows[:, ROWS:], later], axis=1).astype(jnp.bfloat16)


def shifted(pulses):
    count = len(pulses)
    return pl.pallas_call(
        functools.partial(shift_kernel, count),
        out_shape=jax.ShapeDtypeStruct((count, 2, 2 * BLOCKS, 2 * ROWS, 128), jnp.bfloat16),
        in_specs=[VMEM] * count,
        out_specs=VMEM,
        compiler_params=PARAMS,
        name="shift",
    )(*pulses).reshape(count * 4 * BLOCKS, 2 * ROWS, 128)


def kappa_phase(bins):
    turned = 31.0 * bins
    left = turned - 97.0 * jnp.floor((turned + 0.5) * (1.0 / 97.0))
    return left * (2.0 * math.pi / 97.0)


def lists_kernel(group_ref, *refs):
    note_refs, whole_ref, turn_ref = refs[:GROUPS], refs[GROUPS], refs[GROUPS + 1]
    notes = [jnp.concatenate([ref[0], ref[1]], axis=1).astype(jnp.float32) for ref in note_refs]
    rows, chosen, cosines, sines = [], [], [], []
    for slot in range(2):
        pulse = jnp.concatenate([note[slot : slot + 1] for note in notes], axis=0)
        start = jnp.concatenate([note[2 + slot : 3 + slot] for note in notes], axis=0)
        errors = [
            jnp.concatenate([note[at : at + 1] + note[at + 1 : at + 2] + note[at + 2 : at + 3] for note in notes], axis=0)
            for at in (4, 7)
        ]
        rotation = kappa_phase(128.0 * start) - jnp.where(pulse < 0.5, errors[0], errors[1])
        filled = pulse < 1.5
        pair = jnp.floor(0.5 * start)
        rows.append((2.0 * (start - 2.0 * pair) + jnp.minimum(pulse, 1.0)) * BLOCKS + pair)
        chosen.append(pulse)
        cosines.append(jnp.where(filled, jnp.cos(rotation), 0.0))
        sines.append(jnp.where(filled, jnp.sin(rotation), 0.0))
    shift = (TILES - group_ref[0] * PLANE) % TILES
    for parts, ref in ((rows + chosen, whole_ref), (cosines + sines, turn_ref)):
        parts = jnp.concatenate(parts + [jnp.zeros((128 - 4 * GROUPS, TILES), jnp.float32)], axis=0)
        parts = pltpu.roll(parts, shift, 1)[:, :128]
        ref[...] = parts.T[:PLANE].astype(ref.dtype)


def lists(group, pulses):
    note = pl.BlockSpec((2, NOTE_ROWS, 128), lambda i: (BLOCKS, 0, 0))
    out = pl.BlockSpec((PLANE, 128), lambda i: (0, 0))
    return pl.pallas_call(
        lists_kernel,
        grid=(1,),
        out_shape=(
            jax.ShapeDtypeStruct((PLANE, 128), jnp.int32),
            jax.ShapeDtypeStruct((PLANE, 128), jnp.float32),
        ),
        in_specs=[SMEM] + [note] * GROUPS,
        out_specs=(out, out),
        compiler_params=PARAMS,
        name="lists",
    )(group, *pulses)


def phase_kernel(group_ref, rate_ref, known_ref, bins_ref, phase_ref):
    cross = known_ref[8].astype(jnp.float32) + known_ref[9].astype(jnp.float32)
    cross = cross + known_ref[10].astype(jnp.float32)
    for dev in range(GROUPS):
        bins = known_ref[group_ref[dev]].astype(jnp.float32) + 256.0
        angle = kappa_phase(bins) + rate_ref[dev] * cross
        phase_ref[dev, 0] = jnp.cos(angle)
        phase_ref[dev, 1] = jnp.sin(angle)
        bins_ref[dev] = bins.astype(jnp.int32)


def phases(groups, rates, known):
    return pl.pallas_call(
        phase_kernel,
        out_shape=(
            jax.ShapeDtypeStruct((GROUPS, PLANE, PIX), jnp.int32),
            jax.ShapeDtypeStruct((GROUPS, 2, PLANE, PIX), jnp.float32),
        ),
        in_specs=[SMEM, SMEM, VMEM],
        out_specs=(VMEM, VMEM),
        compiler_params=PARAMS,
        name="phases",
    )(groups, rates, known)


def pick_lanes(rows, lanes):
    dims = lax.GatherDimensionNumbers(
        offset_dims=(),
        collapsed_slice_dims=(1,),
        start_index_map=(1,),
        operand_batching_dims=(0,),
        start_indices_batching_dims=(0,),
    )
    return lax.gather(rows, lanes[..., None], dims, slice_sizes=(1, 1), mode="promise_in_bounds")


def image_kernel(whole_ref, turn_ref, bins_ref, phase_ref, comp_a, comp_b, comp_c, part_ref, kept_ref, sum_ref):
    sign = row_sign((ROWS, 128), 0)
    homes = [(comp_a, 0), (comp_a, 1), (comp_b, 0), (comp_b, 1), (comp_b, 2), (comp_b, 3), (comp_c, 0), (comp_c, 1)]

    def step(tile, carry):
        total = [None, None]
        for dev in range(GROUPS):
            comp_ref, home = homes[dev]
            bins = bins_ref[dev, pl.ds(tile, 1), :]
            cos_row = phase_ref[dev, 0, pl.ds(tile, 1), :]
            sin_row = phase_ref[dev, 1, pl.ds(tile, 1), :]
            sources = []
            for slot in range(2):
                base = whole_ref[tile, slot * GROUPS + dev] + home * 4 * BLOCKS
                sources.append((comp_ref[base], comp_ref[base + 1]))
            cos_rot = [turn_ref[tile, slot * GROUPS + dev] for slot in range(2)]
            sin_rot = [turn_ref[tile, (2 + slot) * GROUPS + dev] * sign for slot in range(2)]
            for half in range(2):
                lanes = slice(half * 128, (half + 1) * 128)
                where = jnp.broadcast_to(bins[:, lanes], (ROWS, 128))
                lane = where & 127
                odd = (where & 128) != 0
                high = (where & 256) != 0
                lane = jnp.concatenate([lane, lane], axis=0).astype(jnp.int16)
                turned = []
                for slot in range(2):
                    low, top = [pick_lanes(source, lane).astype(jnp.float32) for source in sources[slot]]
                    value = jnp.where(
                        high, jnp.where(odd, top[ROWS:], top[:ROWS]), jnp.where(odd, low[ROWS:], low[:ROWS])
                    )
                    value = cos_rot[slot] * value + sin_rot[slot] * pltpu.roll(value, POLS, 0)
                    turned.append(value.astype(jnp.bfloat16))
                kept_ref[tile, dev, :, lanes] = jnp.concatenate(turned, axis=0)
                summed = turned[0].astype(jnp.float32) + turned[1].astype(jnp.float32)
                term = jnp.broadcast_to(cos_row[:, lanes], (ROWS, 128)) * summed + jnp.broadcast_to(
                    sin_row[:, lanes], (ROWS, 128)
                ) * (sign * pltpu.roll(summed, POLS, 0))
                total[half] = term if total[half] is None else total[half] + term
        sum_ref[tile] = jnp.concatenate(total, axis=1)
        return carry

    lax.fori_loop(0, PLANE, step, 0)
    part_ref[...] = sum_ref[...].reshape(PLANE * ROWS, PIX).astype(jnp.bfloat16)


def image_parts(whole, turn, bins, phase, comps):
    return pl.pallas_call(
        image_kernel,
        out_shape=(
            jax.ShapeDtypeStruct((PLANE * ROWS, PIX), jnp.bfloat16),
            jax.ShapeDtypeStruct((PLANE, GROUPS, 2 * ROWS, PIX), jnp.bfloat16),
        ),
        in_specs=[SMEM, SMEM] + [VMEM] * 5,
        out_specs=(VMEM, VMEM),
        scratch_shapes=[pltpu.VMEM((PLANE, ROWS, PIX), jnp.float32)],
        compiler_params=PARAMS,
        name="image",
    )(whole, turn, bins, phase, *comps)


def total_kernel(parts_ref, tile_ref, copies_ref):
    image = IMAGE_SCALE * jnp.sum(parts_ref[...].astype(jnp.float32), axis=0)
    for row in range(ROWS):
        tile_ref[row % POLS, row // POLS, :] = image[row]
    for at in range(PLANE):
        copies_ref[at] = image


def total_image(parts):
    return pl.pallas_call(
        total_kernel,
        out_shape=(
            jax.ShapeDtypeStruct((POLS, 2, PIX), jnp.float32),
            jax.ShapeDtypeStruct((PLANE, ROWS, PIX), jnp.float32),
        ),
        in_specs=[VMEM],
        out_specs=(VMEM, VMEM),
        compiler_params=PARAMS,
        name="total",
    )(parts)


def grad_kernel(group_ref, whole_ref, image_ref, kept_ref, phase_ref, out_ref):
    sign = row_sign((ROWS, 128), 0)

    def step(tile, sums):
        sums = list(sums)
        firsts, seconds = [], []
        for half in range(2):
            image = image_ref[tile, :, half * 128 : (half + 1) * 128]
            other = pltpu.roll(image, POLS, 0)
            size = 4.0 * (image * image + other * other)
            firsts.append(size * image)
            seconds.append((size * other) * sign)
        for dev in range(GROUPS):
            cos_row = phase_ref[dev, 0, pl.ds(tile, 1), :]
            sin_row = phase_ref[dev, 1, pl.ds(tile, 1), :]
            weights = []
            for half in range(2):
                lanes = slice(half * 128, (half + 1) * 128)
                weights.append(
                    firsts[half] * jnp.broadcast_to(sin_row[:, lanes], (ROWS, 128))
                    + seconds[half] * jnp.broadcast_to(cos_row[:, lanes], (ROWS, 128))
                )
            kept = kept_ref[tile, dev].astype(jnp.float32)
            for slot in range(2):
                value = kept[slot * ROWS : (slot + 1) * ROWS]
                term = weights[0] * value[:, :128] + weights[1] * value[:, 128:]
                pulse = whole_ref[tile, (2 + slot) * GROUPS + dev]
                for which in range(2):
                    at = dev * 2 + which
                    sums[at] = sums[at] + jnp.where(pulse == which, 1.0, 0.0) * term
        return tuple(sums)

    zero = jnp.zeros((ROWS, 128), jnp.float32)
    sums = lax.fori_loop(0, PLANE, step, (zero,) * (2 * GROUPS))
    lane = lax.broadcasted_iota(jnp.int32, (ROWS, 128), 1)
    for dev in range(GROUPS):
        pair = [jnp.sum(sums[dev * 2 + which], keepdims=True) * GRAD_SCALE for which in range(2)]
        out_ref[group_ref[dev]] = jnp.where(lane == 0, pair[0], pair[1])


def grad_parts(groups, whole, image, kept, phase):
    return pl.pallas_call(
        grad_kernel,
        out_shape=jax.ShapeDtypeStruct((GROUPS, ROWS, 128), jnp.float32),
        in_specs=[SMEM, SMEM] + [VMEM] * 3,
        out_specs=VMEM,
        compiler_params=PARAMS,
        name="grad",
    )(groups, whole, image, kept, phase)


def body(raw_pulses, chirp_taps, phase_error, illumination, swath_start, range_bins, cross_range):
    core = lax.axis_index("core")
    at_y = lax.axis_index("y")
    at_plane = lax.axis_index(("x", "z"))
    groups = jnp.stack([2 * ((at_y + 4 - back) % 4) + (core + other) % 2 for back, other in BLOCK_ORDER])
    rates = math.pi * (2 * (groups * PLANE + at_plane) + 1 - TILES).astype(jnp.float32) / TILES

    raw = raw_pulses.reshape(2, POLS, 2, BLOCKS, BLOCK).transpose(0, 3, 2, 1, 4)
    own, known = compress(
        raw.reshape(2 * BLOCKS * ROWS, BLOCK),
        jnp.pad(chirp_taps, ((0, 0), (0, SPAN - TAPS))),
        phase_error,
        illumination[0].T,
        swath_start[0].T,
        range_bins[0],
        cross_range,
    )
    line = {0: own}
    for back in (1, 3, 2):
        line[back] = lax.ppermute(own, "y", [(at, (at + back) % 4) for at in range(4)])
    known = lax.all_to_all(known, ("x", "z"), 0, 0, tiled=True)
    line[1], line[3], line[2], known = lax.optimization_barrier((line[1], line[3], line[2], known))
    pulses = []
    for back in (0, 1, 3, 2):
        pulses += [line[back], lax.ppermute(line[back], "core", [(0, 1), (1, 0)])]

    bins, phase = phases(groups, rates, known.transpose(1, 0, 2))
    comps = [shifted(pulses[:2]), shifted(pulses[2:6]), shifted(pulses[6:])]
    whole, turn = lists(groups[:1], pulses)

    parts, kept = image_parts(whole, turn, bins, phase, comps)
    parts = lax.all_to_all(parts.reshape(PLANE, ROWS, PIX), ("x", "z"), 0, 0, tiled=True)
    image_tile, copies = total_image(parts)
    images = lax.all_to_all(copies, ("x", "z"), 0, 0, tiled=True)
    grads = grad_parts(groups, whole, images, kept, phase)
    grads = lax.all_to_all(grads, ("y", "core"), 0, 0, tiled=True)
    return (image_tile[None], jnp.sum(grads[:, 0, :2], axis=0))


def solution(mesh):
    fine = Mesh(mesh.devices.reshape(4, 2, 4, 8), ("y", "core", "x", "z"))
    every = ("y", "core", "x", "z")
    return jax.shard_map(
        body,
        mesh=fine,
        in_specs=(
            P(every, None, None, None),
            P(),
            P(every),
            P(every, None, None),
            P(every, None, None),
            P(every, None, None),
            P(every, None),
        ),
        out_specs=(P(every, None, None, None), P(every)),
        check_vma=False,
    )
```

```python
import functools
import math

import jax
import jax.numpy as jnp
from jax import lax
from jax.experimental import pallas as pl
from jax.experimental.pallas import tpu as pltpu
from jax.sharding import Mesh, PartitionSpec as P

TAPS = 1024
RBINS = 16384
POLS = 4
SWATH = 512
PIX = 256
TILES = 256
GROUPS = 8
PLANE = 32
ROWS = 2 * POLS
BLOCK = 256
BLOCKS = RBINS // BLOCK
NOTE_ROWS = 16
EDGE = TAPS // BLOCK * ROWS
SPAN = TAPS + BLOCK
IMAGE_SCALE = 1.0 / math.sqrt(TILES * 2)
GRAD_SCALE = IMAGE_SCALE / math.sqrt(PIX * POLS)
VMEM_LIMIT = 14 * 1024 * 1024
BLOCK_ORDER = ((0, 0), (0, 1), (1, 0), (1, 1), (3, 0), (3, 1), (2, 0), (2, 1))
EARLY = 6
SMEM = pl.BlockSpec(memory_space=pltpu.SMEM)
VMEM = pl.BlockSpec(memory_space=pltpu.VMEM)
PARAMS = pltpu.CompilerParams(vmem_limit_bytes=VMEM_LIMIT)


def row_sign(shape, axis):
    return jnp.where(lax.broadcasted_iota(jnp.int32, shape, axis) < POLS, -1.0, 1.0)


def three_parts(x):
    first = x.astype(jnp.bfloat16).astype(jnp.float32)
    second = (x - first).astype(jnp.bfloat16).astype(jnp.float32)
    return [first, second, x - first - second]


def compress_kernel(
    raw_ref, taps_ref, error_ref, chosen_ref, start_ref, bins_ref, cross_ref, out_ref, known_ref, left_ref, odd_ref
):
    known = [bins_ref[...].astype(jnp.float32) - 256.0] + three_parts(cross_ref[...])
    known.append(jnp.zeros((5, PIX), jnp.float32))
    known = jnp.concatenate(known, axis=0).astype(jnp.bfloat16)
    for at in range(PLANE):
        known_ref[at] = known

    taps = taps_ref[...].astype(jnp.bfloat16).astype(jnp.float32)
    wide = []
    for part in range(2):
        rows = jnp.broadcast_to(taps[part : part + 1], (128, SPAN))
        rows = pltpu.roll(rows, 0, 1, stride=1, stride_axis=0).astype(jnp.bfloat16)
        later = jnp.concatenate([jnp.zeros((128, 128), jnp.bfloat16), rows[:, : SPAN - 128]], axis=1)
        wide.append(jnp.concatenate([rows, later], axis=0))

    total = BLOCKS * ROWS
    stride = total + EDGE
    for pulse in range(2):
        own = raw_ref[pulse * total : (pulse + 1) * total]
        edge = jnp.zeros((EDGE + ROWS, BLOCK), jnp.float32)
        at = pulse * stride
        left_ref[at : at + total] = own
        left_ref[at + total : at + stride] = edge[ROWS:].astype(jnp.bfloat16)
        odd_ref[at : at + stride] = jnp.concatenate([own.astype(jnp.float32)[ROWS:], edge], axis=0).astype(jnp.bfloat16)
    shifted = []
    for j in range(SPAN // BLOCK):
        source = odd_ref if j % 2 else left_ref
        at = j // 2 * 2 * ROWS
        shifted.append(source[at : at + stride + total])
    sums = lax.dot_general(
        jnp.concatenate(shifted, axis=1),
        jnp.concatenate(wide, axis=0),
        (((1,), (1,)), ((), ())),
        preferred_element_type=jnp.float32,
    )
    for pulse in range(2):
        done = sums[pulse * stride : pulse * stride + total].reshape(BLOCKS, ROWS, 2 * BLOCK)
        crossed = pltpu.roll(done[:, :, BLOCK:], POLS, 1) * -row_sign((BLOCKS, ROWS, BLOCK), 1)
        done = done[:, :, :BLOCK] + crossed
        out_ref[pulse * BLOCKS : (pulse + 1) * BLOCKS] = jnp.concatenate(
            [done[:, :, :128], done[:, :, 128:]], axis=1
        ).astype(jnp.bfloat16)

    rows = [chosen_ref[...].astype(jnp.float32), start_ref[...].astype(jnp.float32)]
    for pulse in range(2):
        rows += three_parts(jnp.full((1, PIX), error_ref[pulse], jnp.float32))
    rows.append(jnp.zeros((NOTE_ROWS - 10, PIX), jnp.float32))
    rows = jnp.concatenate(rows, axis=0).astype(jnp.bfloat16)
    out_ref[2 * BLOCKS] = rows[:, :128]
    out_ref[2 * BLOCKS + 1] = rows[:, 128:]


def compress(raw, taps, phase_error, chosen, start, bins, cross):
    return pl.pallas_call(
        compress_kernel,
        out_shape=(
            jax.ShapeDtypeStruct((2 * BLOCKS + 2, 2 * ROWS, 128), jnp.bfloat16),
            jax.ShapeDtypeStruct((PLANE, 16, PIX), jnp.bfloat16),
        ),
        in_specs=[VMEM, VMEM, SMEM, VMEM, VMEM, VMEM, VMEM],
        out_specs=(VMEM, VMEM),
        scratch_shapes=[
            pltpu.VMEM((2 * (BLOCKS * ROWS + EDGE), BLOCK), jnp.bfloat16),
            pltpu.VMEM((2 * (BLOCKS * ROWS + EDGE), BLOCK), jnp.bfloat16),
        ],
        compiler_params=PARAMS,
        name="compress",
    )(raw, taps, phase_error, chosen, start, bins, cross)


def halves_kernel(near_ref, far_ref, first_ref, second_ref):
    first_ref[...] = near_ref[:BLOCKS]
    second_ref[...] = far_ref[BLOCKS:]


def halves(near, far):
    return pl.pallas_call(
        halves_kernel,
        out_shape=(
            jax.ShapeDtypeStruct((BLOCKS, 2 * ROWS, 128), jnp.bfloat16),
            jax.ShapeDtypeStruct((BLOCKS + 2, 2 * ROWS, 128), jnp.bfloat16),
        ),
        in_specs=[VMEM, VMEM],
        out_specs=(VMEM, VMEM),
        compiler_params=PARAMS,
        name="halves",
    )(near, far)


def pieces(refs):
    if len(refs) == 1:
        return [(refs[0], 0), (refs[0], BLOCKS), (refs[0], 2 * BLOCKS)]
    return [(refs[0], 0), (refs[1], 0), (refs[1], BLOCKS)]


def write_pairs(blocks, comp_ref):
    size = 2 * BLOCKS
    for dev, block in enumerate(blocks):
        for pulse in range(2):
            ref, place = block[pulse]
            at = dev * 2 * size + pulse * BLOCKS
            comp_ref[at : at + BLOCKS] = ref[place : place + BLOCKS]
            rows = ref[place : place + BLOCKS].astype(jnp.float32)
            later = jnp.concatenate([rows[1:, :ROWS], rows[:1, :ROWS]], axis=0)
            at = at + size
            comp_ref[at : at + BLOCKS] = jnp.concatenate([rows[:, ROWS:], later], axis=1).astype(jnp.bfloat16)


def kappa_turns(bins):
    turned = 31.0 * bins
    left = turned - 97.0 * jnp.floor((turned + 0.5) * (1.0 / 97.0))
    return left * (1.0 / 97.0)


def cos_sin(turns):
    quarter = jnp.floor(4.0 * turns + 0.5)
    angle = (turns - 0.25 * quarter) * (2.0 * math.pi)
    square = angle * angle
    cosine = 1.0 + square * (-1 / 2 + square * (1 / 24 + square * (-1 / 720 + square * (1 / 40320))))
    sine = 1.0 + square * (-1 / 6 + square * (1 / 120 + square * (-1 / 5040 + square * (1 / 362880))))
    sine = angle * sine
    quarter = quarter.astype(jnp.int32)
    crossed = (quarter & 1) != 0
    first = jnp.where(crossed, sine, cosine)
    second = jnp.where(crossed, cosine, sine)
    first = jnp.where(((quarter + 1) & 2) != 0, -first, first)
    second = jnp.where((quarter & 2) != 0, -second, second)
    return first, second


def write_lists(group, blocks, whole_ref, turn_ref):
    count = len(blocks)
    notes = [
        jnp.concatenate([ref[place], ref[place + 1]], axis=1).astype(jnp.float32) for _, _, (ref, place) in blocks
    ]
    homes = jnp.concatenate([jnp.full((1, PIX), at * 4.0 * BLOCKS, jnp.float32) for at in range(count)], axis=0)
    rows, chosen, cosines, sines = [], [], [], []
    for slot in range(2):
        pulse = jnp.concatenate([note[slot : slot + 1] for note in notes], axis=0)
        start = jnp.concatenate([note[2 + slot : 3 + slot] for note in notes], axis=0)
        errors = [
            jnp.concatenate([note[at : at + 1] + note[at + 1 : at + 2] + note[at + 2 : at + 3] for note in notes], axis=0)
            for at in (4, 7)
        ]
        errors = jnp.where(pulse < 0.5, errors[0], errors[1]) * (0.5 / math.pi)
        cosine, sine = cos_sin(kappa_turns(128.0 * start) - errors)
        filled = pulse < 1.5
        pair = jnp.floor(0.5 * start)
        rows.append((2.0 * (start - 2.0 * pair) + jnp.minimum(pulse, 1.0)) * BLOCKS + pair + homes)
        chosen.append(pulse)
        cosines.append(jnp.where(filled, cosine, 0.0))
        sines.append(jnp.where(filled, sine, 0.0))
    shift = (TILES - group * PLANE) % TILES
    for parts, ref in ((rows + chosen, whole_ref), (cosines + sines, turn_ref)):
        parts = jnp.concatenate(parts + [jnp.zeros((128 - 4 * count, TILES), jnp.float32)], axis=0)
        parts = pltpu.roll(parts, shift, 1)[:, :128]
        ref[...] = parts.T[:PLANE].astype(ref.dtype)


def phase_kernel(group_ref, rate_ref, known_ref, bins_ref, phase_ref, facts_ref):
    facts_ref[...] = jnp.swapaxes(known_ref[...].astype(jnp.float32), 0, 1)
    cross = facts_ref[8] + facts_ref[9] + facts_ref[10]
    for dev in range(GROUPS):
        bins = facts_ref[group_ref[dev]] + 256.0
        phase_ref[dev, 0], phase_ref[dev, 1] = cos_sin(kappa_turns(bins) + rate_ref[dev] * cross)
        bins_ref[dev] = bins.astype(jnp.int32)


def phases(groups, rates, known):
    return pl.pallas_call(
        phase_kernel,
        out_shape=(
            jax.ShapeDtypeStruct((GROUPS, PLANE, PIX), jnp.int32),
            jax.ShapeDtypeStruct((GROUPS, 2, PLANE, PIX), jnp.float32),
        ),
        in_specs=[SMEM, SMEM, VMEM],
        out_specs=(VMEM, VMEM),
        scratch_shapes=[pltpu.VMEM((16, PLANE, PIX), jnp.float32)],
        compiler_params=PARAMS,
        cost_estimate=pl.CostEstimate(flops=1_200_000_000, bytes_accessed=1_000_000, transcendentals=0),
        name="phases",
    )(groups, rates, known)


def pick_lanes(rows, lanes):
    dims = lax.GatherDimensionNumbers(
        offset_dims=(),
        collapsed_slice_dims=(1,),
        start_index_map=(1,),
        operand_batching_dims=(0,),
        start_indices_batching_dims=(0,),
    )
    return lax.gather(rows, lanes[..., None], dims, slice_sizes=(1, 1), mode="promise_in_bounds")


def image_kernel(first, count, parts, last, group_ref, bins_ref, phase_ref, *refs):
    blocks = [pieces(refs[at * parts : (at + 1) * parts]) for at in range(count)]
    refs = refs[count * parts :]
    if first:
        before_ref, refs = refs[0], refs[1:]
    part_ref, kept_ref, lists_ref, comp_ref, turns_ref, whole_ref, turn_ref, sems, *rest = refs
    sum_ref = rest[0] if last else part_ref
    write_lists(group_ref[0], blocks, lists_ref, turns_ref)
    copies = [
        pltpu.make_async_copy(lists_ref, whole_ref, sems.at[0]),
        pltpu.make_async_copy(turns_ref, turn_ref, sems.at[1]),
    ]
    for copy in copies:
        copy.start()
    write_pairs(blocks, comp_ref)
    for copy in copies:
        copy.wait()
    sign = row_sign((ROWS, 128), 0)

    def step(tile, carry):
        total = [before_ref[tile, :, :128], before_ref[tile, :, 128:]] if first else [None, None]
        for at in range(count):
            dev = first + at
            bins = bins_ref[dev, pl.ds(tile, 1), :]
            cos_row = phase_ref[dev, 0, pl.ds(tile, 1), :]
            sin_row = phase_ref[dev, 1, pl.ds(tile, 1), :]
            sources = []
            for slot in range(2):
                base = whole_ref[tile, slot * count + at]
                sources.append((comp_ref[base], comp_ref[base + 1]))
            cos_rot = [turn_ref[tile, slot * count + at] for slot in range(2)]
            sin_rot = [turn_ref[tile, (2 + slot) * count + at] * sign for slot in range(2)]
            for half in range(2):
                lanes = slice(half * 128, (half + 1) * 128)
                where = jnp.broadcast_to(bins[:, lanes], (ROWS, 128))
                lane = where & 127
                odd = (where & 128) != 0
                high = (where & 256) != 0
                lane = jnp.concatenate([lane, lane], axis=0).astype(jnp.int16)
                turned = []
                for slot in range(2):
                    low, top = [pick_lanes(source, lane).astype(jnp.float32) for source in sources[slot]]
                    value = jnp.where(
                        high, jnp.where(odd, top[ROWS:], top[:ROWS]), jnp.where(odd, low[ROWS:], low[:ROWS])
                    )
                    turned.append(cos_rot[slot] * value + sin_rot[slot] * pltpu.roll(value, POLS, 0))
                turned = jnp.concatenate(turned, axis=0).astype(jnp.bfloat16)
                kept_ref[tile, at, :, lanes] = turned
                turned = turned.astype(jnp.float32)
                summed = turned[:ROWS] + turned[ROWS:]
                term = jnp.broadcast_to(cos_row[:, lanes], (ROWS, 128)) * summed + jnp.broadcast_to(
                    sin_row[:, lanes], (ROWS, 128)
                ) * (sign * pltpu.roll(summed, POLS, 0))
                total[half] = term if total[half] is None else total[half] + term
        sum_ref[tile] = jnp.concatenate(total, axis=1)
        return carry

    lax.fori_loop(0, PLANE, step, 0, unroll=8 if last else 4)
    if last:
        part_ref[...] = sum_ref[...].reshape(PLANE * ROWS, PIX).astype(jnp.bfloat16)


def image_parts(first, group, bins, phase, pulses, before=()):
    count, parts = len(pulses), len(pulses[0])
    pulses = [piece for block in pulses for piece in block]
    last = first + count == GROUPS
    part = ((PLANE * ROWS, PIX), jnp.bfloat16) if last else ((PLANE, ROWS, PIX), jnp.float32)
    return pl.pallas_call(
        functools.partial(image_kernel, first, count, parts, last),
        out_shape=(
            jax.ShapeDtypeStruct(*part),
            jax.ShapeDtypeStruct((PLANE, count, 2 * ROWS, PIX), jnp.bfloat16),
            jax.ShapeDtypeStruct((PLANE, 128), jnp.int32),
        ),
        in_specs=[SMEM] + [VMEM] * (2 + len(pulses) + len(before)),
        out_specs=(VMEM, VMEM, VMEM),
        scratch_shapes=[
            pltpu.VMEM((count * 4 * BLOCKS, 2 * ROWS, 128), jnp.bfloat16),
            pltpu.VMEM((PLANE, 128), jnp.float32),
            pltpu.SMEM((PLANE, 128), jnp.int32),
            pltpu.SMEM((PLANE, 128), jnp.float32),
            pltpu.SemaphoreType.DMA((2,)),
        ]
        + ([pltpu.VMEM((PLANE, ROWS, PIX), jnp.float32)] if last else []),
        compiler_params=PARAMS,
        cost_estimate=pl.CostEstimate(flops=100_000_000 * count, bytes_accessed=1_000_000, transcendentals=0),
        name="image",
    )(group, bins, phase, *pulses, *before)


def total_kernel(parts_ref, tile_ref, copies_ref):
    image = IMAGE_SCALE * jnp.sum(parts_ref[...].astype(jnp.float32), axis=0)
    for row in range(ROWS):
        tile_ref[row % POLS, row // POLS, :] = image[row]
    for at in range(PLANE):
        copies_ref[at] = image


def total_image(parts):
    return pl.pallas_call(
        total_kernel,
        out_shape=(
            jax.ShapeDtypeStruct((POLS, 2, PIX), jnp.float32),
            jax.ShapeDtypeStruct((PLANE, ROWS, PIX), jnp.float32),
        ),
        in_specs=[VMEM],
        out_specs=(VMEM, VMEM),
        compiler_params=PARAMS,
        name="total",
    )(parts)


def grad_kernel(group_ref, whole_a, whole_b, image_ref, kept_a, kept_b, phase_ref, out_ref):
    sign = row_sign((ROWS, 128), 0)

    def step(tile, sums):
        sums = list(sums)
        firsts, seconds = [], []
        for half in range(2):
            image = image_ref[tile, :, half * 128 : (half + 1) * 128]
            other = pltpu.roll(image, POLS, 0)
            size = 4.0 * (image * image + other * other)
            firsts.append(size * image)
            seconds.append((size * other) * sign)
        for dev in range(GROUPS):
            cos_row = phase_ref[dev, 0, pl.ds(tile, 1), :]
            sin_row = phase_ref[dev, 1, pl.ds(tile, 1), :]
            weights = []
            for half in range(2):
                lanes = slice(half * 128, (half + 1) * 128)
                weights.append(
                    firsts[half] * jnp.broadcast_to(sin_row[:, lanes], (ROWS, 128))
                    + seconds[half] * jnp.broadcast_to(cos_row[:, lanes], (ROWS, 128))
                )
            whole_ref, kept_ref, at = (whole_a, kept_a, dev) if dev < EARLY else (whole_b, kept_b, dev - EARLY)
            count = EARLY if dev < EARLY else GROUPS - EARLY
            kept = kept_ref[tile, at].astype(jnp.float32)
            for slot in range(2):
                value = kept[slot * ROWS : (slot + 1) * ROWS]
                term = weights[0] * value[:, :128] + weights[1] * value[:, 128:]
                pulse = whole_ref[tile, (2 + slot) * count + at]
                for which in range(2):
                    home = dev * 2 + which
                    sums[home] = sums[home] + jnp.where(pulse == which, 1.0, 0.0) * term
        return tuple(sums)

    zero = jnp.zeros((ROWS, 128), jnp.float32)
    sums = lax.fori_loop(0, PLANE, step, (zero,) * (2 * GROUPS), unroll=4)
    rows = jnp.concatenate([jnp.sum(part, axis=0, keepdims=True) for part in sums], axis=0)
    totals = jnp.sum(rows, axis=1, keepdims=True) * GRAD_SCALE
    lane = lax.broadcasted_iota(jnp.int32, (1, 128), 1)
    for dev in range(GROUPS):
        out_ref[group_ref[dev]] = jnp.where(lane == 0, totals[2 * dev : 2 * dev + 1], totals[2 * dev + 1 : 2 * dev + 2])


def grad_parts(groups, wholes, image, kepts, phase):
    return pl.pallas_call(
        grad_kernel,
        out_shape=jax.ShapeDtypeStruct((GROUPS, 1, 128), jnp.float32),
        in_specs=[SMEM, SMEM, SMEM] + [VMEM] * 4,
        out_specs=VMEM,
        compiler_params=PARAMS,
        name="grad",
    )(groups, *wholes, image, *kepts, phase)


def body(raw_pulses, chirp_taps, phase_error, illumination, swath_start, range_bins, cross_range):
    core = lax.axis_index("core")
    at_y = lax.axis_index("y")
    at_plane = lax.axis_index(("x", "z"))
    groups = jnp.stack([2 * ((at_y + 4 - back) % 4) + (core + other) % 2 for back, other in BLOCK_ORDER])
    rates = (2 * (groups * PLANE + at_plane) + 1 - TILES).astype(jnp.float32) / (2 * TILES)

    raw = raw_pulses.reshape(2, POLS, 2, BLOCKS, BLOCK).transpose(0, 3, 2, 1, 4)
    own, known = compress(
        raw.reshape(2 * BLOCKS * ROWS, BLOCK),
        jnp.pad(chirp_taps, ((0, 0), (0, SPAN - TAPS))),
        phase_error,
        illumination[0].T,
        swath_start[0].T,
        range_bins[0],
        cross_range,
    )
    def back_by(x, steps):
        return lax.ppermute(x, "y", [(at, (at + steps) % 4) for at in range(4)])

    def pair(*block):
        return [block, tuple(lax.ppermute(x, "core", [(0, 1), (1, 0)]) for x in block)]

    near, far = back_by(own, 1), back_by(own, 3)
    first, second = halves(near, far)
    across = (back_by(first, 1), back_by(second, 3))
    known = lax.all_to_all(known, ("x", "z"), 0, 0, tiled=True)
    bins, phase = phases(groups, rates, known)
    before, kept_a, whole_a = image_parts(0, groups[:1], bins, phase, pair(own) + pair(near) + pair(far))
    across = lax.optimization_barrier((*across, before))[:2]
    parts, kept_b, whole_b = image_parts(EARLY, groups[:1], bins, phase, pair(*across), (before,))
    parts = lax.all_to_all(parts.reshape(PLANE, ROWS, PIX), ("x", "z"), 0, 0, tiled=True)
    image_tile, copies = total_image(parts)
    images = lax.all_to_all(copies, ("x", "z"), 0, 0, tiled=True)
    grads = grad_parts(groups, (whole_a, whole_b), images, (kept_a, kept_b), phase)
    grads = lax.all_to_all(grads, ("y", "core"), 0, 0, tiled=True)
    return (image_tile[None], jnp.sum(grads[:, 0, :2], axis=0))


def solution(mesh):
    fine = Mesh(mesh.devices.reshape(4, 2, 4, 8), ("y", "core", "x", "z"))
    every = ("y", "core", "x", "z")
    return jax.shard_map(
        body,
        mesh=fine,
        in_specs=(
            P(every, None, None, None),
            P(),
            P(every),
            P(every, None, None),
            P(every, None, None),
            P(every, None, None),
            P(every, None),
        ),
        out_specs=(P(every, None, None, None), P(every)),
        check_vma=False,
    )
```

```python
import functools
import math

import jax
import jax.numpy as jnp
from jax import lax
from jax.experimental import pallas as pl
from jax.experimental.pallas import tpu as pltpu
from jax.sharding import Mesh, PartitionSpec as P

TAPS = 1024
RBINS = 16384
POLS = 4
SWATH = 512
PIX = 256
TILES = 256
GROUPS = 8
PLANE = 32
ROWS = 2 * POLS
BLOCK = 256
BLOCKS = RBINS // BLOCK
NOTE_ROWS = 16
EDGE = TAPS // BLOCK * ROWS
SPAN = TAPS + BLOCK
IMAGE_SCALE = 1.0 / math.sqrt(TILES * 2)
GRAD_SCALE = IMAGE_SCALE / math.sqrt(PIX * POLS)
VMEM_LIMIT = 14 * 1024 * 1024
BLOCK_ORDER = ((0, 0), (0, 1), (1, 0), (1, 1), (3, 0), (3, 1), (2, 0), (2, 1))
EARLY = 6
SMEM = pl.BlockSpec(memory_space=pltpu.SMEM)
VMEM = pl.BlockSpec(memory_space=pltpu.VMEM)
PARAMS = pltpu.CompilerParams(vmem_limit_bytes=VMEM_LIMIT)


def row_sign(shape, axis):
    return jnp.where(lax.broadcasted_iota(jnp.int32, shape, axis) < POLS, -1.0, 1.0)


def three_parts(x):
    first = x.astype(jnp.bfloat16).astype(jnp.float32)
    second = (x - first).astype(jnp.bfloat16).astype(jnp.float32)
    return [first, second, x - first - second]


def compress_kernel(
    raw_ref, taps_ref, error_ref, chosen_ref, start_ref, bins_ref, cross_ref, out_ref, known_ref, left_ref, odd_ref
):
    known = [bins_ref[...].astype(jnp.float32) - 256.0] + three_parts(cross_ref[...])
    known.append(jnp.zeros((5, PIX), jnp.float32))
    known = jnp.concatenate(known, axis=0).astype(jnp.bfloat16)
    for at in range(PLANE):
        known_ref[at] = known

    taps = taps_ref[...].astype(jnp.bfloat16).astype(jnp.float32)
    wide = []
    for part in range(2):
        rows = jnp.broadcast_to(taps[part : part + 1], (128, SPAN))
        rows = pltpu.roll(rows, 0, 1, stride=1, stride_axis=0).astype(jnp.bfloat16)
        later = jnp.concatenate([jnp.zeros((128, 128), jnp.bfloat16), rows[:, : SPAN - 128]], axis=1)
        wide.append(jnp.concatenate([rows, later], axis=0))

    total = BLOCKS * ROWS
    stride = total + EDGE
    for pulse in range(2):
        own = raw_ref[pulse * total : (pulse + 1) * total]
        edge = jnp.zeros((EDGE + ROWS, BLOCK), jnp.float32)
        at = pulse * stride
        left_ref[at : at + total] = own
        left_ref[at + total : at + stride] = edge[ROWS:].astype(jnp.bfloat16)
        odd_ref[at : at + stride] = jnp.concatenate([own.astype(jnp.float32)[ROWS:], edge], axis=0).astype(jnp.bfloat16)
    shifted = []
    for j in range(SPAN // BLOCK):
        source = odd_ref if j % 2 else left_ref
        at = j // 2 * 2 * ROWS
        shifted.append(source[at : at + stride + total])
    sums = lax.dot_general(
        jnp.concatenate(shifted, axis=1),
        jnp.concatenate(wide, axis=0),
        (((1,), (1,)), ((), ())),
        preferred_element_type=jnp.float32,
    )
    for pulse in range(2):
        done = sums[pulse * stride : pulse * stride + total].reshape(BLOCKS, ROWS, 2 * BLOCK)
        crossed = pltpu.roll(done[:, :, BLOCK:], POLS, 1) * -row_sign((BLOCKS, ROWS, BLOCK), 1)
        done = done[:, :, :BLOCK] + crossed
        out_ref[pulse * BLOCKS : (pulse + 1) * BLOCKS] = jnp.concatenate(
            [done[:, :, :128], done[:, :, 128:]], axis=1
        ).astype(jnp.bfloat16)

    rows = [chosen_ref[...].astype(jnp.float32), start_ref[...].astype(jnp.float32)]
    for pulse in range(2):
        rows += three_parts(jnp.full((1, PIX), error_ref[pulse], jnp.float32))
    rows.append(jnp.zeros((NOTE_ROWS - 10, PIX), jnp.float32))
    rows = jnp.concatenate(rows, axis=0).astype(jnp.bfloat16)
    out_ref[2 * BLOCKS] = rows[:, :128]
    out_ref[2 * BLOCKS + 1] = rows[:, 128:]


def compress(raw, taps, phase_error, chosen, start, bins, cross):
    return pl.pallas_call(
        compress_kernel,
        out_shape=(
            jax.ShapeDtypeStruct((2 * BLOCKS + 2, 2 * ROWS, 128), jnp.bfloat16),
            jax.ShapeDtypeStruct((PLANE, 16, PIX), jnp.bfloat16),
        ),
        in_specs=[VMEM, VMEM, SMEM, VMEM, VMEM, VMEM, VMEM],
        out_specs=(VMEM, VMEM),
        scratch_shapes=[
            pltpu.VMEM((2 * (BLOCKS * ROWS + EDGE), BLOCK), jnp.bfloat16),
            pltpu.VMEM((2 * (BLOCKS * ROWS + EDGE), BLOCK), jnp.bfloat16),
        ],
        compiler_params=PARAMS,
        name="compress",
    )(raw, taps, phase_error, chosen, start, bins, cross)


def onward_kernel(core_ref, near_ref, far_ref, out_ref):
    @pl.when(core_ref[0] == 0)
    def _():
        out_ref[...] = near_ref[...]

    @pl.when(core_ref[0] != 0)
    def _():
        out_ref[...] = far_ref[...]


def onward(core, near, far):
    return pl.pallas_call(
        onward_kernel,
        out_shape=jax.ShapeDtypeStruct(near.shape, near.dtype),
        in_specs=[SMEM, VMEM, VMEM],
        out_specs=VMEM,
        compiler_params=PARAMS,
        name="onward",
    )(core, near, far)


def pieces(refs):
    if len(refs) == 1:
        return [(refs[0], 0), (refs[0], BLOCKS), (refs[0], 2 * BLOCKS)]
    return [(refs[0], 0), (refs[1], 0), (refs[1], BLOCKS)]


def write_pairs(blocks, comp_ref):
    size = 2 * BLOCKS
    for dev, block in enumerate(blocks):
        for pulse in range(2):
            ref, place = block[pulse]
            at = dev * 2 * size + pulse * BLOCKS
            comp_ref[at : at + BLOCKS] = ref[place : place + BLOCKS]
            rows = ref[place : place + BLOCKS].astype(jnp.float32)
            later = jnp.concatenate([rows[1:, :ROWS], rows[:1, :ROWS]], axis=0)
            at = at + size
            comp_ref[at : at + BLOCKS] = jnp.concatenate([rows[:, ROWS:], later], axis=1).astype(jnp.bfloat16)


def kappa_turns(bins):
    turned = 31.0 * bins
    left = turned - 97.0 * jnp.floor((turned + 0.5) * (1.0 / 97.0))
    return left * (1.0 / 97.0)


def cos_sin(turns):
    quarter = jnp.floor(4.0 * turns + 0.5)
    angle = (turns - 0.25 * quarter) * (2.0 * math.pi)
    square = angle * angle
    cosine = 1.0 + square * (-1 / 2 + square * (1 / 24 + square * (-1 / 720 + square * (1 / 40320))))
    sine = 1.0 + square * (-1 / 6 + square * (1 / 120 + square * (-1 / 5040 + square * (1 / 362880))))
    sine = angle * sine
    quarter = quarter.astype(jnp.int32)
    crossed = (quarter & 1) != 0
    first = jnp.where(crossed, sine, cosine)
    second = jnp.where(crossed, cosine, sine)
    first = jnp.where(((quarter + 1) & 2) != 0, -first, first)
    second = jnp.where((quarter & 2) != 0, -second, second)
    return first, second


def write_lists(group, blocks, whole_ref, turn_ref):
    count = len(blocks)
    notes = [
        jnp.concatenate([ref[place], ref[place + 1]], axis=1).astype(jnp.float32) for _, _, (ref, place) in blocks
    ]
    homes = jnp.concatenate([jnp.full((1, PIX), at * 4.0 * BLOCKS, jnp.float32) for at in range(count)], axis=0)
    rows, chosen, cosines, sines = [], [], [], []
    for slot in range(2):
        pulse = jnp.concatenate([note[slot : slot + 1] for note in notes], axis=0)
        start = jnp.concatenate([note[2 + slot : 3 + slot] for note in notes], axis=0)
        errors = [
            jnp.concatenate([note[at : at + 1] + note[at + 1 : at + 2] + note[at + 2 : at + 3] for note in notes], axis=0)
            for at in (4, 7)
        ]
        errors = jnp.where(pulse < 0.5, errors[0], errors[1]) * (0.5 / math.pi)
        cosine, sine = cos_sin(kappa_turns(128.0 * start) - errors)
        filled = pulse < 1.5
        pair = jnp.floor(0.5 * start)
        rows.append((2.0 * (start - 2.0 * pair) + jnp.minimum(pulse, 1.0)) * BLOCKS + pair + homes)
        chosen.append(pulse)
        cosines.append(jnp.where(filled, cosine, 0.0))
        sines.append(jnp.where(filled, sine, 0.0))
    shift = (TILES - group * PLANE) % TILES
    for parts, ref in ((rows + chosen, whole_ref), (cosines + sines, turn_ref)):
        parts = jnp.concatenate(parts + [jnp.zeros((128 - 4 * count, TILES), jnp.float32)], axis=0)
        parts = pltpu.roll(parts, shift, 1)[:, :128]
        ref[...] = parts.T[:PLANE].astype(ref.dtype)


def phase_kernel(group_ref, rate_ref, known_ref, bins_ref, phase_ref, facts_ref):
    facts_ref[...] = jnp.swapaxes(known_ref[...].astype(jnp.float32), 0, 1)
    cross = facts_ref[8] + facts_ref[9] + facts_ref[10]
    for dev in range(GROUPS):
        bins = facts_ref[group_ref[dev]] + 256.0
        phase_ref[dev, 0], phase_ref[dev, 1] = cos_sin(kappa_turns(bins) + rate_ref[dev] * cross)
        bins_ref[dev] = bins.astype(jnp.int32)


def phases(groups, rates, known):
    return pl.pallas_call(
        phase_kernel,
        out_shape=(
            jax.ShapeDtypeStruct((GROUPS, PLANE, PIX), jnp.int32),
            jax.ShapeDtypeStruct((GROUPS, 2, PLANE, PIX), jnp.float32),
        ),
        in_specs=[SMEM, SMEM, VMEM],
        out_specs=(VMEM, VMEM),
        scratch_shapes=[pltpu.VMEM((16, PLANE, PIX), jnp.float32)],
        compiler_params=PARAMS,
        cost_estimate=pl.CostEstimate(flops=1_200_000_000, bytes_accessed=1_000_000, transcendentals=0),
        name="phases",
    )(groups, rates, known)


def pick_lanes(rows, lanes):
    dims = lax.GatherDimensionNumbers(
        offset_dims=(),
        collapsed_slice_dims=(1,),
        start_index_map=(1,),
        operand_batching_dims=(0,),
        start_indices_batching_dims=(0,),
    )
    return lax.gather(rows, lanes[..., None], dims, slice_sizes=(1, 1), mode="promise_in_bounds")


def image_kernel(first, count, parts, last, group_ref, bins_ref, phase_ref, *refs):
    blocks = [pieces(refs[at * parts : (at + 1) * parts]) for at in range(count)]
    refs = refs[count * parts :]
    if first:
        before_ref, refs = refs[0], refs[1:]
    part_ref, kept_ref, lists_ref, comp_ref, turns_ref, whole_ref, turn_ref, sems, *rest = refs
    sum_ref = rest[0] if last else part_ref
    write_lists(group_ref[0], blocks, lists_ref, turns_ref)
    copies = [
        pltpu.make_async_copy(lists_ref, whole_ref, sems.at[0]),
        pltpu.make_async_copy(turns_ref, turn_ref, sems.at[1]),
    ]
    for copy in copies:
        copy.start()
    write_pairs(blocks, comp_ref)
    for copy in copies:
        copy.wait()
    sign = row_sign((ROWS, 128), 0)

    def step(tile, carry):
        total = [before_ref[tile, :, :128], before_ref[tile, :, 128:]] if first else [None, None]
        for at in range(count):
            dev = first + at
            bins = bins_ref[dev, pl.ds(tile, 1), :]
            cos_row = phase_ref[dev, 0, pl.ds(tile, 1), :]
            sin_row = phase_ref[dev, 1, pl.ds(tile, 1), :]
            sources = []
            for slot in range(2):
                base = whole_ref[tile, slot * count + at]
                sources.append((comp_ref[base], comp_ref[base + 1]))
            cos_rot = [turn_ref[tile, slot * count + at] for slot in range(2)]
            sin_rot = [turn_ref[tile, (2 + slot) * count + at] * sign for slot in range(2)]
            for half in range(2):
                lanes = slice(half * 128, (half + 1) * 128)
                where = jnp.broadcast_to(bins[:, lanes], (ROWS, 128))
                lane = where & 127
                odd = (where & 128) != 0
                high = (where & 256) != 0
                lane = jnp.concatenate([lane, lane], axis=0).astype(jnp.int16)
                turned = []
                for slot in range(2):
                    low, top = [pick_lanes(source, lane).astype(jnp.float32) for source in sources[slot]]
                    value = jnp.where(
                        high, jnp.where(odd, top[ROWS:], top[:ROWS]), jnp.where(odd, low[ROWS:], low[:ROWS])
                    )
                    turned.append(cos_rot[slot] * value + sin_rot[slot] * pltpu.roll(value, POLS, 0))
                turned = jnp.concatenate(turned, axis=0).astype(jnp.bfloat16)
                kept_ref[tile, at, :, lanes] = turned
                turned = turned.astype(jnp.float32)
                summed = turned[:ROWS] + turned[ROWS:]
                term = jnp.broadcast_to(cos_row[:, lanes], (ROWS, 128)) * summed + jnp.broadcast_to(
                    sin_row[:, lanes], (ROWS, 128)
                ) * (sign * pltpu.roll(summed, POLS, 0))
                total[half] = term if total[half] is None else total[half] + term
        sum_ref[tile] = jnp.concatenate(total, axis=1)
        return carry

    lax.fori_loop(0, PLANE, step, 0, unroll=8 if last else 4)
    if last:
        part_ref[...] = sum_ref[...].reshape(PLANE * ROWS, PIX).astype(jnp.bfloat16)


def image_parts(first, group, bins, phase, pulses, before=()):
    count, parts = len(pulses), len(pulses[0])
    pulses = [piece for block in pulses for piece in block]
    last = first + count == GROUPS
    part = ((PLANE * ROWS, PIX), jnp.bfloat16) if last else ((PLANE, ROWS, PIX), jnp.float32)
    return pl.pallas_call(
        functools.partial(image_kernel, first, count, parts, last),
        out_shape=(
            jax.ShapeDtypeStruct(*part),
            jax.ShapeDtypeStruct((PLANE, count, 2 * ROWS, PIX), jnp.bfloat16),
            jax.ShapeDtypeStruct((PLANE, 128), jnp.int32),
        ),
        in_specs=[SMEM] + [VMEM] * (2 + len(pulses) + len(before)),
        out_specs=(VMEM, VMEM, VMEM),
        scratch_shapes=[
            pltpu.VMEM((count * 4 * BLOCKS, 2 * ROWS, 128), jnp.bfloat16),
            pltpu.VMEM((PLANE, 128), jnp.float32),
            pltpu.SMEM((PLANE, 128), jnp.int32),
            pltpu.SMEM((PLANE, 128), jnp.float32),
            pltpu.SemaphoreType.DMA((2,)),
        ]
        + ([pltpu.VMEM((PLANE, ROWS, PIX), jnp.float32)] if last else []),
        compiler_params=PARAMS,
        cost_estimate=pl.CostEstimate(flops=100_000_000 * count, bytes_accessed=1_000_000, transcendentals=0),
        name="image",
    )(group, bins, phase, *pulses, *before)


def total_kernel(parts_ref, tile_ref, copies_ref):
    image = IMAGE_SCALE * jnp.sum(parts_ref[...].astype(jnp.float32), axis=0)
    for row in range(ROWS):
        tile_ref[row % POLS, row // POLS, :] = image[row]
    for at in range(PLANE):
        copies_ref[at] = image


def total_image(parts):
    return pl.pallas_call(
        total_kernel,
        out_shape=(
            jax.ShapeDtypeStruct((POLS, 2, PIX), jnp.float32),
            jax.ShapeDtypeStruct((PLANE, ROWS, PIX), jnp.float32),
        ),
        in_specs=[VMEM],
        out_specs=(VMEM, VMEM),
        compiler_params=PARAMS,
        name="total",
    )(parts)


def grad_kernel(group_ref, whole_a, whole_b, image_ref, kept_a, kept_b, phase_ref, out_ref):
    sign = row_sign((ROWS, 128), 0)

    def step(tile, sums):
        sums = list(sums)
        firsts, seconds = [], []
        for half in range(2):
            image = image_ref[tile, :, half * 128 : (half + 1) * 128]
            other = pltpu.roll(image, POLS, 0)
            size = 4.0 * (image * image + other * other)
            firsts.append(size * image)
            seconds.append((size * other) * sign)
        for dev in range(GROUPS):
            cos_row = phase_ref[dev, 0, pl.ds(tile, 1), :]
            sin_row = phase_ref[dev, 1, pl.ds(tile, 1), :]
            weights = []
            for half in range(2):
                lanes = slice(half * 128, (half + 1) * 128)
                weights.append(
                    firsts[half] * jnp.broadcast_to(sin_row[:, lanes], (ROWS, 128))
                    + seconds[half] * jnp.broadcast_to(cos_row[:, lanes], (ROWS, 128))
                )
            whole_ref, kept_ref, at = (whole_a, kept_a, dev) if dev < EARLY else (whole_b, kept_b, dev - EARLY)
            count = EARLY if dev < EARLY else GROUPS - EARLY
            kept = kept_ref[tile, at].astype(jnp.float32)
            for slot in range(2):
                value = kept[slot * ROWS : (slot + 1) * ROWS]
                term = weights[0] * value[:, :128] + weights[1] * value[:, 128:]
                pulse = whole_ref[tile, (2 + slot) * count + at]
                for which in range(2):
                    home = dev * 2 + which
                    sums[home] = sums[home] + jnp.where(pulse == which, 1.0, 0.0) * term
        return tuple(sums)

    zero = jnp.zeros((ROWS, 128), jnp.float32)
    sums = lax.fori_loop(0, PLANE, step, (zero,) * (2 * GROUPS), unroll=4)
    rows = jnp.concatenate([jnp.sum(part, axis=0, keepdims=True) for part in sums], axis=0)
    totals = jnp.sum(rows, axis=1, keepdims=True) * GRAD_SCALE
    lane = lax.broadcasted_iota(jnp.int32, (1, 128), 1)
    for dev in range(GROUPS):
        out_ref[group_ref[dev]] = jnp.where(lane == 0, totals[2 * dev : 2 * dev + 1], totals[2 * dev + 1 : 2 * dev + 2])


def grad_parts(groups, wholes, image, kepts, phase):
    return pl.pallas_call(
        grad_kernel,
        out_shape=jax.ShapeDtypeStruct((GROUPS, 1, 128), jnp.float32),
        in_specs=[SMEM, SMEM, SMEM] + [VMEM] * 4,
        out_specs=VMEM,
        compiler_params=PARAMS,
        name="grad",
    )(groups, *wholes, image, *kepts, phase)


def body(raw_pulses, chirp_taps, phase_error, illumination, swath_start, range_bins, cross_range):
    core = lax.axis_index("core")
    at_y = lax.axis_index("y")
    at_plane = lax.axis_index(("x", "z"))
    groups = jnp.stack([2 * ((at_y + 4 - back) % 4) + (core + other) % 2 for back, other in BLOCK_ORDER])
    rates = (2 * (groups * PLANE + at_plane) + 1 - TILES).astype(jnp.float32) / (2 * TILES)

    raw = raw_pulses.reshape(2, POLS, 2, BLOCKS, BLOCK).transpose(0, 3, 2, 1, 4)
    own, known = compress(
        raw.reshape(2 * BLOCKS * ROWS, BLOCK),
        jnp.pad(chirp_taps, ((0, 0), (0, SPAN - TAPS))),
        phase_error,
        illumination[0].T,
        swath_start[0].T,
        range_bins[0],
        cross_range,
    )
    def back_by(x, steps):
        return lax.ppermute(x, "y", [(at, (at + steps) % 4) for at in range(4)])

    def pair(*block):
        return [block, tuple(lax.ppermute(x, "core", [(0, 1), (1, 0)]) for x in block)]

    near, far = back_by(own, 1), back_by(own, 3)
    across = lax.ppermute(
        onward(core.reshape(1), near, far),
        ("y", "core"),
        [(2 * at, 2 * ((at + 1) % 4)) for at in range(4)] + [(2 * at + 1, 2 * ((at + 3) % 4) + 1) for at in range(4)],
    )
    known = lax.all_to_all(known, ("x", "z"), 0, 0, tiled=True)
    bins, phase = phases(groups, rates, known)
    before, kept_a, whole_a = image_parts(0, groups[:1], bins, phase, pair(own) + pair(near) + pair(far))
    across = lax.optimization_barrier((across, before))[0]
    parts, kept_b, whole_b = image_parts(EARLY, groups[:1], bins, phase, pair(across), (before,))
    parts = lax.all_to_all(parts.reshape(PLANE, ROWS, PIX), ("x", "z"), 0, 0, tiled=True)
    image_tile, copies = total_image(parts)
    images = lax.all_to_all(copies, ("x", "z"), 0, 0, tiled=True)
    grads = grad_parts(groups, (whole_a, whole_b), images, (kept_a, kept_b), phase)
    grads = lax.all_to_all(grads, ("y", "core"), 0, 0, tiled=True)
    return (image_tile[None], jnp.sum(grads[:, 0, :2], axis=0))


def solution(mesh):
    fine = Mesh(mesh.devices.reshape(4, 2, 4, 8), ("y", "core", "x", "z"))
    every = ("y", "core", "x", "z")
    return jax.shard_map(
        body,
        mesh=fine,
        in_specs=(
            P(every, None, None, None),
            P(),
            P(every),
            P(every, None, None),
            P(every, None, None),
            P(every, None, None),
            P(every, None),
        ),
        out_specs=(P(every, None, None, None), P(every)),
        check_vma=False,
    )
```

```python
import functools
import math

import jax
import jax.numpy as jnp
from jax import lax
from jax.experimental import pallas as pl
from jax.experimental.pallas import tpu as pltpu
from jax.sharding import Mesh, PartitionSpec as P

TAPS = 1024
RBINS = 16384
POLS = 4
SWATH = 512
PIX = 256
TILES = 256
GROUPS = 8
PLANE = 32
ROWS = 2 * POLS
BLOCK = 256
BLOCKS = RBINS // BLOCK
NOTE_ROWS = 16
EDGE = TAPS // BLOCK * ROWS
SPAN = TAPS + BLOCK
IMAGE_SCALE = 1.0 / math.sqrt(TILES * 2)
GRAD_SCALE = IMAGE_SCALE / math.sqrt(PIX * POLS)
VMEM_LIMIT = 14 * 1024 * 1024
BLOCK_ORDER = ((0, 0), (0, 1), (1, 0), (1, 1), (3, 0), (3, 1), (2, 0), (2, 1))
EARLY = 6
SMEM = pl.BlockSpec(memory_space=pltpu.SMEM)
VMEM = pl.BlockSpec(memory_space=pltpu.VMEM)
PARAMS = pltpu.CompilerParams(vmem_limit_bytes=VMEM_LIMIT)


def row_sign(shape, axis):
    return jnp.where(lax.broadcasted_iota(jnp.int32, shape, axis) < POLS, -1.0, 1.0)


def three_parts(x):
    first = x.astype(jnp.bfloat16).astype(jnp.float32)
    second = (x - first).astype(jnp.bfloat16).astype(jnp.float32)
    return [first, second, x - first - second]


def compress_kernel(
    raw_ref, taps_ref, error_ref, chosen_ref, start_ref, bins_ref, cross_ref, out_ref, known_ref, left_ref, odd_ref
):
    known = [bins_ref[...].astype(jnp.float32) - 256.0] + three_parts(cross_ref[...])
    known.append(jnp.zeros((5, PIX), jnp.float32))
    known = jnp.concatenate(known, axis=0).astype(jnp.bfloat16)
    for at in range(PLANE):
        known_ref[at] = known

    taps = taps_ref[...].astype(jnp.bfloat16).astype(jnp.float32)
    wide = []
    for part in range(2):
        rows = jnp.broadcast_to(taps[part : part + 1], (128, SPAN))
        rows = pltpu.roll(rows, 0, 1, stride=1, stride_axis=0).astype(jnp.bfloat16)
        later = jnp.concatenate([jnp.zeros((128, 128), jnp.bfloat16), rows[:, : SPAN - 128]], axis=1)
        wide.append(jnp.concatenate([rows, later], axis=0))

    total = BLOCKS * ROWS
    stride = total + EDGE
    for pulse in range(2):
        own = raw_ref[pulse * total : (pulse + 1) * total]
        edge = jnp.zeros((EDGE + ROWS, BLOCK), jnp.float32)
        at = pulse * stride
        left_ref[at : at + total] = own
        left_ref[at + total : at + stride] = edge[ROWS:].astype(jnp.bfloat16)
        odd_ref[at : at + stride] = jnp.concatenate([own.astype(jnp.float32)[ROWS:], edge], axis=0).astype(jnp.bfloat16)
    shifted = []
    for j in range(SPAN // BLOCK):
        source = odd_ref if j % 2 else left_ref
        at = j // 2 * 2 * ROWS
        shifted.append(source[at : at + stride + total])
    sums = lax.dot_general(
        jnp.concatenate(shifted, axis=1),
        jnp.concatenate(wide, axis=0),
        (((1,), (1,)), ((), ())),
        preferred_element_type=jnp.float32,
    )
    for pulse in range(2):
        done = sums[pulse * stride : pulse * stride + total].reshape(BLOCKS, ROWS, 2 * BLOCK)
        crossed = pltpu.roll(done[:, :, BLOCK:], POLS, 1) * -row_sign((BLOCKS, ROWS, BLOCK), 1)
        done = done[:, :, :BLOCK] + crossed
        out_ref[pulse * BLOCKS : (pulse + 1) * BLOCKS] = jnp.concatenate(
            [done[:, :, :128], done[:, :, 128:]], axis=1
        ).astype(jnp.bfloat16)

    rows = [chosen_ref[...].astype(jnp.float32), start_ref[...].astype(jnp.float32)]
    for pulse in range(2):
        rows += three_parts(jnp.full((1, PIX), error_ref[pulse], jnp.float32))
    rows.append(jnp.zeros((NOTE_ROWS - 10, PIX), jnp.float32))
    rows = jnp.concatenate(rows, axis=0).astype(jnp.bfloat16)
    out_ref[2 * BLOCKS] = rows[:, :128]
    out_ref[2 * BLOCKS + 1] = rows[:, 128:]


def compress(raw, taps, phase_error, chosen, start, bins, cross):
    return pl.pallas_call(
        compress_kernel,
        out_shape=(
            jax.ShapeDtypeStruct((2 * BLOCKS + 2, 2 * ROWS, 128), jnp.bfloat16),
            jax.ShapeDtypeStruct((PLANE, 16, PIX), jnp.bfloat16),
        ),
        in_specs=[VMEM, VMEM, SMEM, VMEM, VMEM, VMEM, VMEM],
        out_specs=(VMEM, VMEM),
        scratch_shapes=[
            pltpu.VMEM((2 * (BLOCKS * ROWS + EDGE), BLOCK), jnp.bfloat16),
            pltpu.VMEM((2 * (BLOCKS * ROWS + EDGE), BLOCK), jnp.bfloat16),
        ],
        compiler_params=PARAMS,
        name="compress",
    )(raw, taps, phase_error, chosen, start, bins, cross)


def onward_kernel(core_ref, near_ref, far_ref, out_ref):
    @pl.when(core_ref[0] == 0)
    def _():
        out_ref[...] = near_ref[...]

    @pl.when(core_ref[0] != 0)
    def _():
        out_ref[...] = far_ref[...]


def onward(core, near, far):
    return pl.pallas_call(
        onward_kernel,
        out_shape=jax.ShapeDtypeStruct(near.shape, near.dtype),
        in_specs=[SMEM, VMEM, VMEM],
        out_specs=VMEM,
        compiler_params=PARAMS,
        name="onward",
    )(core, near, far)


def fetch_kernel(block_ref, out_ref):
    out_ref[...] = block_ref[...]


def fetched(block):
    return pl.pallas_call(
        fetch_kernel,
        out_shape=jax.ShapeDtypeStruct(block.shape, block.dtype),
        in_specs=[VMEM],
        out_specs=VMEM,
        compiler_params=PARAMS,
        cost_estimate=pl.CostEstimate(flops=1_200_000_000, bytes_accessed=4_000_000, transcendentals=0),
        name="fetch",
    )(block)


def pieces(refs):
    if len(refs) == 1:
        return [(refs[0], 0), (refs[0], BLOCKS), (refs[0], 2 * BLOCKS)]
    return [(refs[0], 0), (refs[1], 0), (refs[1], BLOCKS)]


def write_pairs(blocks, comp_ref):
    size = 2 * BLOCKS
    for dev, block in enumerate(blocks):
        for pulse in range(2):
            ref, place = block[pulse]
            at = dev * 2 * size + pulse * BLOCKS
            comp_ref[at : at + BLOCKS] = ref[place : place + BLOCKS]
            rows = ref[place : place + BLOCKS].astype(jnp.float32)
            later = jnp.concatenate([rows[1:, :ROWS], rows[:1, :ROWS]], axis=0)
            at = at + size
            comp_ref[at : at + BLOCKS] = jnp.concatenate([rows[:, ROWS:], later], axis=1).astype(jnp.bfloat16)


def kappa_turns(bins):
    turned = 31.0 * bins
    left = turned - 97.0 * jnp.floor((turned + 0.5) * (1.0 / 97.0))
    return left * (1.0 / 97.0)


def cos_sin(turns):
    quarter = jnp.floor(4.0 * turns + 0.5)
    angle = (turns - 0.25 * quarter) * (2.0 * math.pi)
    square = angle * angle
    cosine = 1.0 + square * (-1 / 2 + square * (1 / 24 + square * (-1 / 720 + square * (1 / 40320))))
    sine = 1.0 + square * (-1 / 6 + square * (1 / 120 + square * (-1 / 5040 + square * (1 / 362880))))
    sine = angle * sine
    quarter = quarter.astype(jnp.int32)
    crossed = (quarter & 1) != 0
    first = jnp.where(crossed, sine, cosine)
    second = jnp.where(crossed, cosine, sine)
    first = jnp.where(((quarter + 1) & 2) != 0, -first, first)
    second = jnp.where((quarter & 2) != 0, -second, second)
    return first, second


def write_lists(group, blocks, whole_ref, turn_ref):
    count = len(blocks)
    notes = [
        jnp.concatenate([ref[place], ref[place + 1]], axis=1).astype(jnp.float32) for _, _, (ref, place) in blocks
    ]
    homes = jnp.concatenate([jnp.full((1, PIX), at * 4.0 * BLOCKS, jnp.float32) for at in range(count)], axis=0)
    rows, chosen, cosines, sines = [], [], [], []
    for slot in range(2):
        pulse = jnp.concatenate([note[slot : slot + 1] for note in notes], axis=0)
        start = jnp.concatenate([note[2 + slot : 3 + slot] for note in notes], axis=0)
        errors = [
            jnp.concatenate([note[at : at + 1] + note[at + 1 : at + 2] + note[at + 2 : at + 3] for note in notes], axis=0)
            for at in (4, 7)
        ]
        errors = jnp.where(pulse < 0.5, errors[0], errors[1]) * (0.5 / math.pi)
        cosine, sine = cos_sin(kappa_turns(128.0 * start) - errors)
        filled = pulse < 1.5
        pair = jnp.floor(0.5 * start)
        rows.append((2.0 * (start - 2.0 * pair) + jnp.minimum(pulse, 1.0)) * BLOCKS + pair + homes)
        chosen.append(pulse)
        cosines.append(jnp.where(filled, cosine, 0.0))
        sines.append(jnp.where(filled, sine, 0.0))
    shift = (TILES - group * PLANE) % TILES
    for parts, ref in ((rows + chosen, whole_ref), (cosines + sines, turn_ref)):
        parts = jnp.concatenate(parts + [jnp.zeros((128 - 4 * count, TILES), jnp.float32)], axis=0)
        parts = pltpu.roll(parts, shift, 1)[:, :128]
        ref[...] = parts.T[:PLANE].astype(ref.dtype)


def phase_kernel(group_ref, rate_ref, known_ref, bins_ref, phase_ref, facts_ref):
    facts_ref[...] = jnp.swapaxes(known_ref[...].astype(jnp.float32), 0, 1)
    cross = facts_ref[8] + facts_ref[9] + facts_ref[10]
    for dev in range(GROUPS):
        bins = facts_ref[group_ref[dev]] + 256.0
        phase_ref[dev, 0], phase_ref[dev, 1] = cos_sin(kappa_turns(bins) + rate_ref[dev] * cross)
        bins_ref[dev] = bins.astype(jnp.int32)


def phases(groups, rates, known):
    return pl.pallas_call(
        phase_kernel,
        out_shape=(
            jax.ShapeDtypeStruct((GROUPS, PLANE, PIX), jnp.int32),
            jax.ShapeDtypeStruct((GROUPS, 2, PLANE, PIX), jnp.float32),
        ),
        in_specs=[SMEM, SMEM, VMEM],
        out_specs=(VMEM, VMEM),
        scratch_shapes=[pltpu.VMEM((16, PLANE, PIX), jnp.float32)],
        compiler_params=PARAMS,
        cost_estimate=pl.CostEstimate(flops=1_200_000_000, bytes_accessed=1_000_000, transcendentals=0),
        name="phases",
    )(groups, rates, known)


def pick_lanes(rows, lanes):
    dims = lax.GatherDimensionNumbers(
        offset_dims=(),
        collapsed_slice_dims=(1,),
        start_index_map=(1,),
        operand_batching_dims=(0,),
        start_indices_batching_dims=(0,),
    )
    return lax.gather(rows, lanes[..., None], dims, slice_sizes=(1, 1), mode="promise_in_bounds")


def image_kernel(first, count, parts, last, group_ref, bins_ref, phase_ref, *refs):
    blocks = [pieces(refs[at * parts : (at + 1) * parts]) for at in range(count)]
    refs = refs[count * parts :]
    if first:
        before_ref, refs = refs[0], refs[1:]
    part_ref, kept_ref, lists_ref, comp_ref, turns_ref, whole_ref, turn_ref, sems, *rest = refs
    sum_ref = rest[0] if last else part_ref
    write_lists(group_ref[0], blocks, lists_ref, turns_ref)
    copies = [
        pltpu.make_async_copy(lists_ref, whole_ref, sems.at[0]),
        pltpu.make_async_copy(turns_ref, turn_ref, sems.at[1]),
    ]
    for copy in copies:
        copy.start()
    write_pairs(blocks, comp_ref)
    for copy in copies:
        copy.wait()
    sign = row_sign((ROWS, 128), 0)

    def step(tile, carry):
        total = [before_ref[tile, :, :128], before_ref[tile, :, 128:]] if first else [None, None]
        for at in range(count):
            dev = first + at
            bins = bins_ref[dev, pl.ds(tile, 1), :]
            cos_row = phase_ref[dev, 0, pl.ds(tile, 1), :]
            sin_row = phase_ref[dev, 1, pl.ds(tile, 1), :]
            sources = []
            for slot in range(2):
                base = whole_ref[tile, slot * count + at]
                sources.append((comp_ref[base], comp_ref[base + 1]))
            cos_rot = [turn_ref[tile, slot * count + at] for slot in range(2)]
            sin_rot = [turn_ref[tile, (2 + slot) * count + at] * sign for slot in range(2)]
            for half in range(2):
                lanes = slice(half * 128, (half + 1) * 128)
                where = jnp.broadcast_to(bins[:, lanes], (ROWS, 128))
                lane = where & 127
                odd = (where & 128) != 0
                high = (where & 256) != 0
                lane = jnp.concatenate([lane, lane], axis=0).astype(jnp.int16)
                turned = []
                for slot in range(2):
                    low, top = [pick_lanes(source, lane).astype(jnp.float32) for source in sources[slot]]
                    value = jnp.where(
                        high, jnp.where(odd, top[ROWS:], top[:ROWS]), jnp.where(odd, low[ROWS:], low[:ROWS])
                    )
                    turned.append(cos_rot[slot] * value + sin_rot[slot] * pltpu.roll(value, POLS, 0))
                turned = jnp.concatenate(turned, axis=0).astype(jnp.bfloat16)
                kept_ref[tile, at, :, lanes] = turned
                turned = turned.astype(jnp.float32)
                summed = turned[:ROWS] + turned[ROWS:]
                term = jnp.broadcast_to(cos_row[:, lanes], (ROWS, 128)) * summed + jnp.broadcast_to(
                    sin_row[:, lanes], (ROWS, 128)
                ) * (sign * pltpu.roll(summed, POLS, 0))
                total[half] = term if total[half] is None else total[half] + term
        sum_ref[tile] = jnp.concatenate(total, axis=1)
        return carry

    lax.fori_loop(0, PLANE, step, 0, unroll=8 if last else 4)
    if last:
        part_ref[...] = sum_ref[...].reshape(PLANE * ROWS, PIX).astype(jnp.bfloat16)


def image_parts(first, group, bins, phase, pulses, before=()):
    count, parts = len(pulses), len(pulses[0])
    pulses = [piece for block in pulses for piece in block]
    last = first + count == GROUPS
    part = ((PLANE * ROWS, PIX), jnp.bfloat16) if last else ((PLANE, ROWS, PIX), jnp.float32)
    return pl.pallas_call(
        functools.partial(image_kernel, first, count, parts, last),
        out_shape=(
            jax.ShapeDtypeStruct(*part),
            jax.ShapeDtypeStruct((PLANE, count, 2 * ROWS, PIX), jnp.bfloat16),
            jax.ShapeDtypeStruct((PLANE, 128), jnp.int32),
        ),
        in_specs=[SMEM] + [VMEM] * (2 + len(pulses) + len(before)),
        out_specs=(VMEM, VMEM, VMEM),
        scratch_shapes=[
            pltpu.VMEM((count * 4 * BLOCKS, 2 * ROWS, 128), jnp.bfloat16),
            pltpu.VMEM((PLANE, 128), jnp.float32),
            pltpu.SMEM((PLANE, 128), jnp.int32),
            pltpu.SMEM((PLANE, 128), jnp.float32),
            pltpu.SemaphoreType.DMA((2,)),
        ]
        + ([pltpu.VMEM((PLANE, ROWS, PIX), jnp.float32)] if last else []),
        compiler_params=PARAMS,
        cost_estimate=pl.CostEstimate(flops=100_000_000 * count, bytes_accessed=1_000_000, transcendentals=0),
        name="image",
    )(group, bins, phase, *pulses, *before)


def total_kernel(parts_ref, tile_ref, copies_ref):
    image = IMAGE_SCALE * jnp.sum(parts_ref[...].astype(jnp.float32), axis=0)
    for row in range(ROWS):
        tile_ref[row % POLS, row // POLS, :] = image[row]
    for at in range(PLANE):
        copies_ref[at] = image


def total_image(parts):
    return pl.pallas_call(
        total_kernel,
        out_shape=(
            jax.ShapeDtypeStruct((POLS, 2, PIX), jnp.float32),
            jax.ShapeDtypeStruct((PLANE, ROWS, PIX), jnp.float32),
        ),
        in_specs=[VMEM],
        out_specs=(VMEM, VMEM),
        compiler_params=PARAMS,
        name="total",
    )(parts)


def grad_kernel(group_ref, whole_a, whole_b, image_ref, kept_a, kept_b, phase_ref, out_ref):
    sign = row_sign((ROWS, 128), 0)

    def step(tile, sums):
        sums = list(sums)
        firsts, seconds = [], []
        for half in range(2):
            image = image_ref[tile, :, half * 128 : (half + 1) * 128]
            other = pltpu.roll(image, POLS, 0)
            size = 4.0 * (image * image + other * other)
            firsts.append(size * image)
            seconds.append((size * other) * sign)
        for dev in range(GROUPS):
            cos_row = phase_ref[dev, 0, pl.ds(tile, 1), :]
            sin_row = phase_ref[dev, 1, pl.ds(tile, 1), :]
            weights = []
            for half in range(2):
                lanes = slice(half * 128, (half + 1) * 128)
                weights.append(
                    firsts[half] * jnp.broadcast_to(sin_row[:, lanes], (ROWS, 128))
                    + seconds[half] * jnp.broadcast_to(cos_row[:, lanes], (ROWS, 128))
                )
            whole_ref, kept_ref, at = (whole_a, kept_a, dev) if dev < EARLY else (whole_b, kept_b, dev - EARLY)
            count = EARLY if dev < EARLY else GROUPS - EARLY
            kept = kept_ref[tile, at].astype(jnp.float32)
            for slot in range(2):
                value = kept[slot * ROWS : (slot + 1) * ROWS]
                term = weights[0] * value[:, :128] + weights[1] * value[:, 128:]
                pulse = whole_ref[tile, (2 + slot) * count + at]
                for which in range(2):
                    home = dev * 2 + which
                    sums[home] = sums[home] + jnp.where(pulse == which, 1.0, 0.0) * term
        return tuple(sums)

    zero = jnp.zeros((ROWS, 128), jnp.float32)
    sums = lax.fori_loop(0, PLANE, step, (zero,) * (2 * GROUPS), unroll=4)
    rows = jnp.concatenate([jnp.sum(part, axis=0, keepdims=True) for part in sums], axis=0)
    totals = jnp.sum(rows, axis=1, keepdims=True) * GRAD_SCALE
    lane = lax.broadcasted_iota(jnp.int32, (1, 128), 1)
    for dev in range(GROUPS):
        out_ref[group_ref[dev]] = jnp.where(lane == 0, totals[2 * dev : 2 * dev + 1], totals[2 * dev + 1 : 2 * dev + 2])


def grad_parts(groups, wholes, image, kepts, phase):
    return pl.pallas_call(
        grad_kernel,
        out_shape=jax.ShapeDtypeStruct((GROUPS, 1, 128), jnp.float32),
        in_specs=[SMEM, SMEM, SMEM] + [VMEM] * 4,
        out_specs=VMEM,
        compiler_params=PARAMS,
        name="grad",
    )(groups, *wholes, image, *kepts, phase)


def body(raw_pulses, chirp_taps, phase_error, illumination, swath_start, range_bins, cross_range):
    core = lax.axis_index("core")
    at_y = lax.axis_index("y")
    at_plane = lax.axis_index(("x", "z"))
    groups = jnp.stack([2 * ((at_y + 4 - back) % 4) + (core + other) % 2 for back, other in BLOCK_ORDER])
    rates = (2 * (groups * PLANE + at_plane) + 1 - TILES).astype(jnp.float32) / (2 * TILES)

    raw = raw_pulses.reshape(2, POLS, 2, BLOCKS, BLOCK).transpose(0, 3, 2, 1, 4)
    own, known = compress(
        raw.reshape(2 * BLOCKS * ROWS, BLOCK),
        jnp.pad(chirp_taps, ((0, 0), (0, SPAN - TAPS))),
        phase_error,
        illumination[0].T,
        swath_start[0].T,
        range_bins[0],
        cross_range,
    )
    def back_by(x, steps):
        return lax.ppermute(x, "y", [(at, (at + steps) % 4) for at in range(4)])

    def pair(*block):
        return [block, tuple(lax.ppermute(x, "core", [(0, 1), (1, 0)]) for x in block)]

    near, far = back_by(own, 1), back_by(own, 3)
    across = lax.ppermute(
        onward(core.reshape(1), near, far),
        ("y", "core"),
        [(2 * at, 2 * ((at + 1) % 4)) for at in range(4)] + [(2 * at + 1, 2 * ((at + 3) % 4) + 1) for at in range(4)],
    )
    known = lax.all_to_all(known, ("x", "z"), 0, 0, tiled=True)
    bins, phase = phases(groups, rates, known)
    before, kept_a, whole_a = image_parts(0, groups[:1], bins, phase, pair(own) + pair(near) + pair(far))
    across = lax.optimization_barrier((across, before))[0]
    pulses = pair(across)
    pulses[0] = (fetched(across),)
    parts, kept_b, whole_b = image_parts(EARLY, groups[:1], bins, phase, pulses, (before,))
    parts = lax.all_to_all(parts.reshape(PLANE, ROWS, PIX), ("x", "z"), 0, 0, tiled=True)
    image_tile, copies = total_image(parts)
    images = lax.all_to_all(copies, ("x", "z"), 0, 0, tiled=True)
    grads = grad_parts(groups, (whole_a, whole_b), images, (kept_a, kept_b), phase)
    grads = lax.all_to_all(grads, ("y", "core"), 0, 0, tiled=True)
    return (image_tile[None], jnp.sum(grads[:, 0, :2], axis=0))


def solution(mesh):
    fine = Mesh(mesh.devices.reshape(4, 2, 4, 8), ("y", "core", "x", "z"))
    every = ("y", "core", "x", "z")
    return jax.shard_map(
        body,
        mesh=fine,
        in_specs=(
            P(every, None, None, None),
            P(),
            P(every),
            P(every, None, None),
            P(every, None, None),
            P(every, None, None),
            P(every, None),
        ),
        out_specs=(P(every, None, None, None), P(every)),
        check_vma=False,
    )
```

```python
import functools
import math

import jax
import jax.numpy as jnp
from jax import lax
from jax.experimental import pallas as pl
from jax.experimental.pallas import tpu as pltpu
from jax.sharding import Mesh, PartitionSpec as P

TAPS = 1024
RBINS = 16384
POLS = 4
SWATH = 512
PIX = 256
TILES = 256
GROUPS = 8
PLANE = 32
ROWS = 2 * POLS
BLOCK = 256
BLOCKS = RBINS // BLOCK
NOTE_ROWS = 16
EDGE = TAPS // BLOCK * ROWS
SPAN = TAPS + BLOCK
IMAGE_SCALE = 1.0 / math.sqrt(TILES * 2)
GRAD_SCALE = IMAGE_SCALE / math.sqrt(PIX * POLS)
VMEM_LIMIT = 14 * 1024 * 1024
BLOCK_ORDER = ((0, 0), (0, 1), (1, 0), (1, 1), (3, 0), (3, 1), (2, 0), (2, 1))
EARLY = 6
SMEM = pl.BlockSpec(memory_space=pltpu.SMEM)
VMEM = pl.BlockSpec(memory_space=pltpu.VMEM)
PARAMS = pltpu.CompilerParams(vmem_limit_bytes=VMEM_LIMIT)


def row_sign(shape, axis):
    return jnp.where(lax.broadcasted_iota(jnp.int32, shape, axis) < POLS, -1.0, 1.0)


def three_parts(x):
    first = x.astype(jnp.bfloat16).astype(jnp.float32)
    second = (x - first).astype(jnp.bfloat16).astype(jnp.float32)
    return [first, second, x - first - second]


def compress_kernel(
    raw_ref,
    taps_ref,
    error_hbm,
    chosen_hbm,
    start_hbm,
    bins_hbm,
    cross_hbm,
    out_ref,
    known_ref,
    left_ref,
    odd_ref,
    error_ref,
    chosen_ref,
    start_ref,
    bins_ref,
    cross_ref,
    sems,
):
    copies = [
        pltpu.make_async_copy(source, target, sems.at[at])
        for at, (source, target) in enumerate(
            ((error_hbm, error_ref), (chosen_hbm, chosen_ref), (start_hbm, start_ref), (bins_hbm, bins_ref), (cross_hbm, cross_ref))
        )
    ]
    for copy in copies:
        copy.start()

    taps = taps_ref[...].astype(jnp.bfloat16).astype(jnp.float32)
    wide = []
    for part in range(2):
        rows = jnp.broadcast_to(taps[part : part + 1], (128, SPAN))
        rows = pltpu.roll(rows, 0, 1, stride=1, stride_axis=0).astype(jnp.bfloat16)
        later = jnp.concatenate([jnp.zeros((128, 128), jnp.bfloat16), rows[:, : SPAN - 128]], axis=1)
        wide.append(jnp.concatenate([rows, later], axis=0))

    total = BLOCKS * ROWS
    stride = total + EDGE
    for pulse in range(2):
        own = raw_ref[pulse * total : (pulse + 1) * total]
        edge = jnp.zeros((EDGE + ROWS, BLOCK), jnp.float32)
        at = pulse * stride
        left_ref[at : at + total] = own
        left_ref[at + total : at + stride] = edge[ROWS:].astype(jnp.bfloat16)
        odd_ref[at : at + stride] = jnp.concatenate([own.astype(jnp.float32)[ROWS:], edge], axis=0).astype(jnp.bfloat16)
    shifted = []
    for j in range(SPAN // BLOCK):
        source = odd_ref if j % 2 else left_ref
        at = j // 2 * 2 * ROWS
        shifted.append(source[at : at + stride + total])
    sums = lax.dot_general(
        jnp.concatenate(shifted, axis=1),
        jnp.concatenate(wide, axis=0),
        (((1,), (1,)), ((), ())),
        preferred_element_type=jnp.float32,
    )
    for pulse in range(2):
        done = sums[pulse * stride : pulse * stride + total].reshape(BLOCKS, ROWS, 2 * BLOCK)
        crossed = pltpu.roll(done[:, :, BLOCK:], POLS, 1) * -row_sign((BLOCKS, ROWS, BLOCK), 1)
        done = done[:, :, :BLOCK] + crossed
        out_ref[pulse * BLOCKS : (pulse + 1) * BLOCKS] = jnp.concatenate(
            [done[:, :, :128], done[:, :, 128:]], axis=1
        ).astype(jnp.bfloat16)

    for copy in copies:
        copy.wait()
    known = [bins_ref[...].astype(jnp.float32) - 256.0] + three_parts(cross_ref[...])
    known.append(jnp.zeros((5, PIX), jnp.float32))
    known = jnp.concatenate(known, axis=0).astype(jnp.bfloat16)
    for at in range(PLANE):
        known_ref[at] = known

    rows = [chosen_ref[...].astype(jnp.float32), start_ref[...].astype(jnp.float32)]
    for pulse in range(2):
        rows += three_parts(jnp.full((1, PIX), error_ref[pulse], jnp.float32))
    rows.append(jnp.zeros((NOTE_ROWS - 10, PIX), jnp.float32))
    rows = jnp.concatenate(rows, axis=0).astype(jnp.bfloat16)
    out_ref[2 * BLOCKS] = rows[:, :128]
    out_ref[2 * BLOCKS + 1] = rows[:, 128:]


def compress(raw, taps, phase_error, chosen, start, bins, cross):
    return pl.pallas_call(
        compress_kernel,
        out_shape=(
            jax.ShapeDtypeStruct((2 * BLOCKS + 2, 2 * ROWS, 128), jnp.bfloat16),
            jax.ShapeDtypeStruct((PLANE, 16, PIX), jnp.bfloat16),
        ),
        in_specs=[VMEM, VMEM] + [pl.BlockSpec(memory_space=pl.ANY)] * 5,
        out_specs=(VMEM, VMEM),
        scratch_shapes=[
            pltpu.VMEM((2 * (BLOCKS * ROWS + EDGE), BLOCK), jnp.bfloat16),
            pltpu.VMEM((2 * (BLOCKS * ROWS + EDGE), BLOCK), jnp.bfloat16),
            pltpu.SMEM(phase_error.shape, jnp.float32),
            pltpu.VMEM(chosen.shape, jnp.int32),
            pltpu.VMEM(start.shape, jnp.int32),
            pltpu.VMEM(bins.shape, jnp.int32),
            pltpu.VMEM(cross.shape, jnp.float32),
            pltpu.SemaphoreType.DMA((5,)),
        ],
        compiler_params=PARAMS,
        name="compress",
    )(raw, taps, phase_error, chosen, start, bins, cross)


def onward_kernel(core_ref, near_ref, far_ref, out_ref):
    @pl.when(core_ref[0] == 0)
    def _():
        out_ref[...] = near_ref[...]

    @pl.when(core_ref[0] != 0)
    def _():
        out_ref[...] = far_ref[...]


def onward(core, near, far):
    return pl.pallas_call(
        onward_kernel,
        out_shape=jax.ShapeDtypeStruct(near.shape, near.dtype),
        in_specs=[SMEM, VMEM, VMEM],
        out_specs=VMEM,
        compiler_params=PARAMS,
        name="onward",
    )(core, near, far)


def fetch_kernel(block_ref, out_ref):
    out_ref[...] = block_ref[...]


def fetched(block):
    return pl.pallas_call(
        fetch_kernel,
        out_shape=jax.ShapeDtypeStruct(block.shape, block.dtype),
        in_specs=[VMEM],
        out_specs=VMEM,
        compiler_params=PARAMS,
        cost_estimate=pl.CostEstimate(flops=1_200_000_000, bytes_accessed=4_000_000, transcendentals=0),
        name="fetch",
    )(block)


def pieces(refs):
    if len(refs) == 1:
        return [(refs[0], 0), (refs[0], BLOCKS), (refs[0], 2 * BLOCKS)]
    return [(refs[0], 0), (refs[1], 0), (refs[1], BLOCKS)]


def write_pairs(blocks, comp_ref):
    size = 2 * BLOCKS
    for dev, block in enumerate(blocks):
        for pulse in range(2):
            ref, place = block[pulse]
            at = dev * 2 * size + pulse * BLOCKS
            comp_ref[at : at + BLOCKS] = ref[place : place + BLOCKS]
            rows = ref[place : place + BLOCKS].astype(jnp.float32)
            later = jnp.concatenate([rows[1:, :ROWS], rows[:1, :ROWS]], axis=0)
            at = at + size
            comp_ref[at : at + BLOCKS] = jnp.concatenate([rows[:, ROWS:], later], axis=1).astype(jnp.bfloat16)


def kappa_turns(bins):
    turned = 31.0 * bins
    left = turned - 97.0 * jnp.floor((turned + 0.5) * (1.0 / 97.0))
    return left * (1.0 / 97.0)


def cos_sin(turns):
    quarter = jnp.floor(4.0 * turns + 0.5)
    angle = (turns - 0.25 * quarter) * (2.0 * math.pi)
    square = angle * angle
    cosine = 1.0 + square * (-1 / 2 + square * (1 / 24 + square * (-1 / 720 + square * (1 / 40320))))
    sine = 1.0 + square * (-1 / 6 + square * (1 / 120 + square * (-1 / 5040 + square * (1 / 362880))))
    sine = angle * sine
    quarter = quarter.astype(jnp.int32)
    crossed = (quarter & 1) != 0
    first = jnp.where(crossed, sine, cosine)
    second = jnp.where(crossed, cosine, sine)
    first = jnp.where(((quarter + 1) & 2) != 0, -first, first)
    second = jnp.where((quarter & 2) != 0, -second, second)
    return first, second


def write_lists(group, blocks, whole_ref, turn_ref):
    count = len(blocks)
    notes = [
        jnp.concatenate([ref[place], ref[place + 1]], axis=1).astype(jnp.float32) for _, _, (ref, place) in blocks
    ]
    homes = jnp.concatenate([jnp.full((1, PIX), at * 4.0 * BLOCKS, jnp.float32) for at in range(count)], axis=0)
    rows, chosen, cosines, sines = [], [], [], []
    for slot in range(2):
        pulse = jnp.concatenate([note[slot : slot + 1] for note in notes], axis=0)
        start = jnp.concatenate([note[2 + slot : 3 + slot] for note in notes], axis=0)
        errors = [
            jnp.concatenate([note[at : at + 1] + note[at + 1 : at + 2] + note[at + 2 : at + 3] for note in notes], axis=0)
            for at in (4, 7)
        ]
        errors = jnp.where(pulse < 0.5, errors[0], errors[1]) * (0.5 / math.pi)
        cosine, sine = cos_sin(kappa_turns(128.0 * start) - errors)
        filled = pulse < 1.5
        pair = jnp.floor(0.5 * start)
        rows.append((2.0 * (start - 2.0 * pair) + jnp.minimum(pulse, 1.0)) * BLOCKS + pair + homes)
        chosen.append(pulse)
        cosines.append(jnp.where(filled, cosine, 0.0))
        sines.append(jnp.where(filled, sine, 0.0))
    shift = (TILES - group * PLANE) % TILES
    for parts, ref in ((rows + chosen, whole_ref), (cosines + sines, turn_ref)):
        parts = jnp.concatenate(parts + [jnp.zeros((128 - 4 * count, TILES), jnp.float32)], axis=0)
        parts = pltpu.roll(parts, shift, 1)[:, :128]
        ref[...] = parts.T[:PLANE].astype(ref.dtype)


def phase_kernel(group_ref, rate_ref, known_ref, bins_ref, phase_ref, facts_ref):
    facts_ref[...] = jnp.swapaxes(known_ref[...].astype(jnp.float32), 0, 1)
    cross = facts_ref[8] + facts_ref[9] + facts_ref[10]
    for dev in range(GROUPS):
        bins = facts_ref[group_ref[dev]] + 256.0
        phase_ref[dev, 0], phase_ref[dev, 1] = cos_sin(kappa_turns(bins) + rate_ref[dev] * cross)
        bins_ref[dev] = bins.astype(jnp.int32)


def phases(groups, rates, known):
    return pl.pallas_call(
        phase_kernel,
        out_shape=(
            jax.ShapeDtypeStruct((GROUPS, PLANE, PIX), jnp.int32),
            jax.ShapeDtypeStruct((GROUPS, 2, PLANE, PIX), jnp.float32),
        ),
        in_specs=[SMEM, SMEM, VMEM],
        out_specs=(VMEM, VMEM),
        scratch_shapes=[pltpu.VMEM((16, PLANE, PIX), jnp.float32)],
        compiler_params=PARAMS,
        cost_estimate=pl.CostEstimate(flops=1_200_000_000, bytes_accessed=1_000_000, transcendentals=0),
        name="phases",
    )(groups, rates, known)


def pick_lanes(rows, lanes):
    dims = lax.GatherDimensionNumbers(
        offset_dims=(),
        collapsed_slice_dims=(1,),
        start_index_map=(1,),
        operand_batching_dims=(0,),
        start_indices_batching_dims=(0,),
    )
    return lax.gather(rows, lanes[..., None], dims, slice_sizes=(1, 1), mode="promise_in_bounds")


def image_kernel(first, count, parts, last, group_ref, bins_ref, phase_ref, *refs):
    blocks = [pieces(refs[at * parts : (at + 1) * parts]) for at in range(count)]
    refs = refs[count * parts :]
    if first:
        before_ref, refs = refs[0], refs[1:]
    part_ref, kept_ref, lists_ref, comp_ref, turns_ref, whole_ref, turn_ref, sems, *rest = refs
    sum_ref = rest[0] if last else part_ref
    write_lists(group_ref[0], blocks, lists_ref, turns_ref)
    copies = [
        pltpu.make_async_copy(lists_ref, whole_ref, sems.at[0]),
        pltpu.make_async_copy(turns_ref, turn_ref, sems.at[1]),
    ]
    for copy in copies:
        copy.start()
    write_pairs(blocks, comp_ref)
    for copy in copies:
        copy.wait()
    sign = row_sign((ROWS, 128), 0)

    def step(tile, carry):
        total = [before_ref[tile, :, :128], before_ref[tile, :, 128:]] if first else [None, None]
        for at in range(count):
            dev = first + at
            bins = bins_ref[dev, pl.ds(tile, 1), :]
            cos_row = phase_ref[dev, 0, pl.ds(tile, 1), :]
            sin_row = phase_ref[dev, 1, pl.ds(tile, 1), :]
            sources = []
            for slot in range(2):
                base = whole_ref[tile, slot * count + at]
                sources.append((comp_ref[base], comp_ref[base + 1]))
            cos_rot = [turn_ref[tile, slot * count + at] for slot in range(2)]
            sin_rot = [turn_ref[tile, (2 + slot) * count + at] * sign for slot in range(2)]
            for half in range(2):
                lanes = slice(half * 128, (half + 1) * 128)
                where = jnp.broadcast_to(bins[:, lanes], (ROWS, 128))
                lane = where & 127
                odd = (where & 128) != 0
                high = (where & 256) != 0
                lane = jnp.concatenate([lane, lane], axis=0).astype(jnp.int16)
                turned = []
                for slot in range(2):
                    low, top = [pick_lanes(source, lane).astype(jnp.float32) for source in sources[slot]]
                    value = jnp.where(
                        high, jnp.where(odd, top[ROWS:], top[:ROWS]), jnp.where(odd, low[ROWS:], low[:ROWS])
                    )
                    turned.append(cos_rot[slot] * value + sin_rot[slot] * pltpu.roll(value, POLS, 0))
                turned = jnp.concatenate(turned, axis=0).astype(jnp.bfloat16)
                kept_ref[tile, at, :, lanes] = turned
                turned = turned.astype(jnp.float32)
                summed = turned[:ROWS] + turned[ROWS:]
                term = jnp.broadcast_to(cos_row[:, lanes], (ROWS, 128)) * summed + jnp.broadcast_to(
                    sin_row[:, lanes], (ROWS, 128)
                ) * (sign * pltpu.roll(summed, POLS, 0))
                total[half] = term if total[half] is None else total[half] + term
        sum_ref[tile] = jnp.concatenate(total, axis=1)
        return carry

    lax.fori_loop(0, PLANE, step, 0, unroll=8)
    if last:
        part_ref[...] = sum_ref[...].reshape(PLANE * ROWS, PIX).astype(jnp.bfloat16)


def image_parts(first, group, bins, phase, pulses, before=()):
    count, parts = len(pulses), len(pulses[0])
    pulses = [piece for block in pulses for piece in block]
    last = first + count == GROUPS
    part = ((PLANE * ROWS, PIX), jnp.bfloat16) if last else ((PLANE, ROWS, PIX), jnp.float32)
    return pl.pallas_call(
        functools.partial(image_kernel, first, count, parts, last),
        out_shape=(
            jax.ShapeDtypeStruct(*part),
            jax.ShapeDtypeStruct((PLANE, count, 2 * ROWS, PIX), jnp.bfloat16),
            jax.ShapeDtypeStruct((PLANE, 128), jnp.int32),
        ),
        in_specs=[SMEM] + [VMEM] * (2 + len(pulses) + len(before)),
        out_specs=(VMEM, VMEM, VMEM),
        scratch_shapes=[
            pltpu.VMEM((count * 4 * BLOCKS, 2 * ROWS, 128), jnp.bfloat16),
            pltpu.VMEM((PLANE, 128), jnp.float32),
            pltpu.SMEM((PLANE, 128), jnp.int32),
            pltpu.SMEM((PLANE, 128), jnp.float32),
            pltpu.SemaphoreType.DMA((2,)),
        ]
        + ([pltpu.VMEM((PLANE, ROWS, PIX), jnp.float32)] if last else []),
        compiler_params=PARAMS,
        cost_estimate=pl.CostEstimate(flops=100_000_000 * count, bytes_accessed=1_000_000, transcendentals=0),
        name="image",
    )(group, bins, phase, *pulses, *before)


def total_kernel(parts_ref, tile_ref, copies_ref):
    image = IMAGE_SCALE * jnp.sum(parts_ref[...].astype(jnp.float32), axis=0)
    for row in range(ROWS):
        tile_ref[row % POLS, row // POLS, :] = image[row]
    for at in range(PLANE):
        copies_ref[at] = image


def total_image(parts):
    return pl.pallas_call(
        total_kernel,
        out_shape=(
            jax.ShapeDtypeStruct((POLS, 2, PIX), jnp.float32),
            jax.ShapeDtypeStruct((PLANE, ROWS, PIX), jnp.float32),
        ),
        in_specs=[VMEM],
        out_specs=(VMEM, VMEM),
        compiler_params=PARAMS,
        name="total",
    )(parts)


def grad_kernel(group_ref, whole_a, whole_b, image_ref, kept_a, kept_b, phase_ref, out_ref):
    sign = row_sign((ROWS, 128), 0)

    def step(tile, sums):
        sums = list(sums)
        firsts, seconds = [], []
        for half in range(2):
            image = image_ref[tile, :, half * 128 : (half + 1) * 128]
            other = pltpu.roll(image, POLS, 0)
            size = 4.0 * (image * image + other * other)
            firsts.append(size * image)
            seconds.append((size * other) * sign)
        for dev in range(GROUPS):
            cos_row = phase_ref[dev, 0, pl.ds(tile, 1), :]
            sin_row = phase_ref[dev, 1, pl.ds(tile, 1), :]
            weights = []
            for half in range(2):
                lanes = slice(half * 128, (half + 1) * 128)
                weights.append(
                    firsts[half] * jnp.broadcast_to(sin_row[:, lanes], (ROWS, 128))
                    + seconds[half] * jnp.broadcast_to(cos_row[:, lanes], (ROWS, 128))
                )
            whole_ref, kept_ref, at = (whole_a, kept_a, dev) if dev < EARLY else (whole_b, kept_b, dev - EARLY)
            count = EARLY if dev < EARLY else GROUPS - EARLY
            kept = kept_ref[tile, at].astype(jnp.float32)
            for slot in range(2):
                value = kept[slot * ROWS : (slot + 1) * ROWS]
                term = weights[0] * value[:, :128] + weights[1] * value[:, 128:]
                pulse = whole_ref[tile, (2 + slot) * count + at]
                for which in range(2):
                    home = dev * 2 + which
                    sums[home] = sums[home] + jnp.where(pulse == which, 1.0, 0.0) * term
        return tuple(sums)

    zero = jnp.zeros((ROWS, 128), jnp.float32)
    sums = lax.fori_loop(0, PLANE, step, (zero,) * (2 * GROUPS), unroll=4)
    rows = jnp.concatenate([jnp.sum(part, axis=0, keepdims=True) for part in sums], axis=0)
    totals = jnp.sum(rows, axis=1, keepdims=True) * GRAD_SCALE
    lane = lax.broadcasted_iota(jnp.int32, (1, 128), 1)
    for dev in range(GROUPS):
        out_ref[group_ref[dev]] = jnp.where(lane == 0, totals[2 * dev : 2 * dev + 1], totals[2 * dev + 1 : 2 * dev + 2])


def grad_parts(groups, wholes, image, kepts, phase):
    return pl.pallas_call(
        grad_kernel,
        out_shape=jax.ShapeDtypeStruct((GROUPS, 1, 128), jnp.float32),
        in_specs=[SMEM, SMEM, SMEM] + [VMEM] * 4,
        out_specs=VMEM,
        compiler_params=PARAMS,
        name="grad",
    )(groups, *wholes, image, *kepts, phase)


def body(raw_pulses, chirp_taps, phase_error, illumination, swath_start, range_bins, cross_range):
    core = lax.axis_index("core")
    at_y = lax.axis_index("y")
    at_plane = lax.axis_index(("x", "z"))
    groups = jnp.stack([2 * ((at_y + 4 - back) % 4) + (core + other) % 2 for back, other in BLOCK_ORDER])
    rates = (2 * (groups * PLANE + at_plane) + 1 - TILES).astype(jnp.float32) / (2 * TILES)

    raw = raw_pulses.reshape(2, POLS, 2, BLOCKS, BLOCK).transpose(0, 3, 2, 1, 4)
    own, known = compress(
        raw.reshape(2 * BLOCKS * ROWS, BLOCK),
        jnp.pad(chirp_taps, ((0, 0), (0, SPAN - TAPS))),
        phase_error,
        illumination[0].T,
        swath_start[0].T,
        range_bins[0],
        cross_range,
    )
    def back_by(x, steps):
        return lax.ppermute(x, "y", [(at, (at + steps) % 4) for at in range(4)])

    def pair(*block):
        return [block, tuple(lax.ppermute(x, "core", [(0, 1), (1, 0)]) for x in block)]

    near, far = back_by(own, 1), back_by(own, 3)
    across = lax.ppermute(
        onward(core.reshape(1), near, far),
        ("y", "core"),
        [(2 * at, 2 * ((at + 1) % 4)) for at in range(4)] + [(2 * at + 1, 2 * ((at + 3) % 4) + 1) for at in range(4)],
    )
    known = lax.all_to_all(known, ("x", "z"), 0, 0, tiled=True)
    bins, phase = phases(groups, rates, known)
    before, kept_a, whole_a = image_parts(0, groups[:1], bins, phase, pair(own) + pair(near) + pair(far))
    across = lax.optimization_barrier((across, before))[0]
    pulses = pair(across)
    pulses[0] = (fetched(across),)
    parts, kept_b, whole_b = image_parts(EARLY, groups[:1], bins, phase, pulses, (before,))
    parts = lax.all_to_all(parts.reshape(PLANE, ROWS, PIX), ("x", "z"), 0, 0, tiled=True)
    image_tile, copies = total_image(parts)
    images = lax.all_to_all(copies, ("x", "z"), 0, 0, tiled=True)
    grads = grad_parts(groups, (whole_a, whole_b), images, (kept_a, kept_b), phase)
    grads = lax.all_to_all(grads, ("y", "core"), 0, 0, tiled=True)
    return (image_tile[None], jnp.sum(grads[:, 0, :2], axis=0))


def solution(mesh):
    fine = Mesh(mesh.devices.reshape(4, 2, 4, 8), ("y", "core", "x", "z"))
    every = ("y", "core", "x", "z")
    return jax.shard_map(
        body,
        mesh=fine,
        in_specs=(
            P(every, None, None, None),
            P(),
            P(every),
            P(every, None, None),
            P(every, None, None),
            P(every, None, None),
            P(every, None),
        ),
        out_specs=(P(every, None, None, None), P(every)),
        check_vma=False,
    )
```

```python
import functools
import math

import jax
import jax.numpy as jnp
from jax import lax
from jax.experimental import pallas as pl
from jax.experimental.pallas import tpu as pltpu
from jax.sharding import Mesh, PartitionSpec as P

TAPS = 1024
RBINS = 16384
POLS = 4
SWATH = 512
PIX = 256
TILES = 256
GROUPS = 8
PLANE = 32
ROWS = 2 * POLS
BLOCK = 256
BLOCKS = RBINS // BLOCK
NOTE_ROWS = 16
EDGE = TAPS // BLOCK * ROWS
SPAN = TAPS + BLOCK
IMAGE_SCALE = 1.0 / math.sqrt(TILES * 2)
GRAD_SCALE = IMAGE_SCALE / math.sqrt(PIX * POLS)
VMEM_LIMIT = 14 * 1024 * 1024
BLOCK_ORDER = ((0, 0), (0, 1), (1, 0), (1, 1), (3, 0), (3, 1), (2, 0), (2, 1))
EARLY = 6
SMEM = pl.BlockSpec(memory_space=pltpu.SMEM)
VMEM = pl.BlockSpec(memory_space=pltpu.VMEM)
PARAMS = pltpu.CompilerParams(vmem_limit_bytes=VMEM_LIMIT)


def row_sign(shape, axis):
    return jnp.where(lax.broadcasted_iota(jnp.int32, shape, axis) < POLS, -1.0, 1.0)


def three_parts(x):
    first = x.astype(jnp.bfloat16).astype(jnp.float32)
    second = (x - first).astype(jnp.bfloat16).astype(jnp.float32)
    return [first, second, x - first - second]


def compress_kernel(
    raw_ref,
    taps_ref,
    error_hbm,
    chosen_hbm,
    start_hbm,
    bins_hbm,
    cross_hbm,
    out_ref,
    known_ref,
    left_ref,
    odd_ref,
    error_ref,
    chosen_ref,
    start_ref,
    bins_ref,
    cross_ref,
    sems,
):
    copies = [
        pltpu.make_async_copy(source, target, sems.at[at])
        for at, (source, target) in enumerate(
            ((error_hbm, error_ref), (chosen_hbm, chosen_ref), (start_hbm, start_ref), (bins_hbm, bins_ref), (cross_hbm, cross_ref))
        )
    ]
    for copy in copies:
        copy.start()

    taps = taps_ref[...].astype(jnp.bfloat16).astype(jnp.float32)
    wide = []
    for part in range(2):
        rows = jnp.broadcast_to(taps[part : part + 1], (128, SPAN))
        rows = pltpu.roll(rows, 0, 1, stride=1, stride_axis=0).astype(jnp.bfloat16)
        later = jnp.concatenate([jnp.zeros((128, 128), jnp.bfloat16), rows[:, : SPAN - 128]], axis=1)
        wide.append(jnp.concatenate([rows, later], axis=0))

    total = BLOCKS * ROWS
    stride = total + EDGE
    for pulse in range(2):
        own = raw_ref[pulse * total : (pulse + 1) * total]
        edge = jnp.zeros((EDGE + ROWS, BLOCK), jnp.float32)
        at = pulse * stride
        left_ref[at : at + total] = own
        left_ref[at + total : at + stride] = edge[ROWS:].astype(jnp.bfloat16)
        odd_ref[at : at + stride] = jnp.concatenate([own.astype(jnp.float32)[ROWS:], edge], axis=0).astype(jnp.bfloat16)
    shifted = []
    for j in range(SPAN // BLOCK):
        source = odd_ref if j % 2 else left_ref
        at = j // 2 * 2 * ROWS
        shifted.append(source[at : at + stride + total])
    sums = lax.dot_general(
        jnp.concatenate(shifted, axis=1),
        jnp.concatenate(wide, axis=0),
        (((1,), (1,)), ((), ())),
        preferred_element_type=jnp.float32,
    )
    for pulse in range(2):
        done = sums[pulse * stride : pulse * stride + total].reshape(BLOCKS, ROWS, 2 * BLOCK)
        crossed = pltpu.roll(done[:, :, BLOCK:], POLS, 1) * -row_sign((BLOCKS, ROWS, BLOCK), 1)
        done = done[:, :, :BLOCK] + crossed
        out_ref[pulse * BLOCKS : (pulse + 1) * BLOCKS] = jnp.concatenate(
            [done[:, :, :128], done[:, :, 128:]], axis=1
        ).astype(jnp.bfloat16)

    for copy in copies:
        copy.wait()
    known = [bins_ref[...].astype(jnp.float32) - 256.0] + three_parts(cross_ref[...])
    known.append(jnp.zeros((5, PIX), jnp.float32))
    known = jnp.concatenate(known, axis=0).astype(jnp.bfloat16)
    for at in range(PLANE):
        known_ref[at] = known

    rows = [chosen_ref[...].astype(jnp.float32), start_ref[...].astype(jnp.float32)]
    for pulse in range(2):
        rows += three_parts(jnp.full((1, PIX), error_ref[pulse], jnp.float32))
    rows.append(jnp.zeros((NOTE_ROWS - 10, PIX), jnp.float32))
    rows = jnp.concatenate(rows, axis=0).astype(jnp.bfloat16)
    out_ref[2 * BLOCKS] = rows[:, :128]
    out_ref[2 * BLOCKS + 1] = rows[:, 128:]


def compress(raw, taps, phase_error, chosen, start, bins, cross):
    return pl.pallas_call(
        compress_kernel,
        out_shape=(
            jax.ShapeDtypeStruct((2 * BLOCKS + 2, 2 * ROWS, 128), jnp.bfloat16),
            jax.ShapeDtypeStruct((PLANE, 16, PIX), jnp.bfloat16),
        ),
        in_specs=[VMEM, VMEM] + [pl.BlockSpec(memory_space=pl.ANY)] * 5,
        out_specs=(VMEM, VMEM),
        scratch_shapes=[
            pltpu.VMEM((2 * (BLOCKS * ROWS + EDGE), BLOCK), jnp.bfloat16),
            pltpu.VMEM((2 * (BLOCKS * ROWS + EDGE), BLOCK), jnp.bfloat16),
            pltpu.SMEM(phase_error.shape, jnp.float32),
            pltpu.VMEM(chosen.shape, jnp.int32),
            pltpu.VMEM(start.shape, jnp.int32),
            pltpu.VMEM(bins.shape, jnp.int32),
            pltpu.VMEM(cross.shape, jnp.float32),
            pltpu.SemaphoreType.DMA((5,)),
        ],
        compiler_params=PARAMS,
        name="compress",
    )(raw, taps, phase_error, chosen, start, bins, cross)


def onward_kernel(core_ref, near_ref, far_ref, out_ref):
    @pl.when(core_ref[0] == 0)
    def _():
        out_ref[...] = near_ref[...]

    @pl.when(core_ref[0] != 0)
    def _():
        out_ref[...] = far_ref[...]


def onward(core, near, far):
    return pl.pallas_call(
        onward_kernel,
        out_shape=jax.ShapeDtypeStruct(near.shape, near.dtype),
        in_specs=[SMEM, VMEM, VMEM],
        out_specs=VMEM,
        compiler_params=PARAMS,
        name="onward",
    )(core, near, far)


def fetch_kernel(block_ref, out_ref):
    out_ref[...] = block_ref[...]


def fetched(block):
    return pl.pallas_call(
        fetch_kernel,
        out_shape=jax.ShapeDtypeStruct(block.shape, block.dtype),
        in_specs=[VMEM],
        out_specs=VMEM,
        compiler_params=PARAMS,
        cost_estimate=pl.CostEstimate(flops=1_200_000_000, bytes_accessed=4_000_000, transcendentals=0),
        name="fetch",
    )(block)


def pieces(refs):
    if len(refs) == 1:
        return [(refs[0], 0), (refs[0], BLOCKS), (refs[0], 2 * BLOCKS)]
    return [(refs[0], 0), (refs[1], 0), (refs[1], BLOCKS)]


def write_pairs(blocks, comp_ref):
    size = 2 * BLOCKS
    for dev, block in enumerate(blocks):
        for pulse in range(2):
            ref, place = block[pulse]
            at = dev * 2 * size + pulse * BLOCKS
            comp_ref[at : at + BLOCKS] = ref[place : place + BLOCKS]
            rows = ref[place : place + BLOCKS].astype(jnp.float32)
            later = jnp.concatenate([rows[1:, :ROWS], rows[:1, :ROWS]], axis=0)
            at = at + size
            comp_ref[at : at + BLOCKS] = jnp.concatenate([rows[:, ROWS:], later], axis=1).astype(jnp.bfloat16)


def kappa_turns(bins):
    turned = 31.0 * bins
    left = turned - 97.0 * jnp.floor((turned + 0.5) * (1.0 / 97.0))
    return left * (1.0 / 97.0)


def cos_sin(turns):
    quarter = jnp.floor(4.0 * turns + 0.5)
    angle = (turns - 0.25 * quarter) * (2.0 * math.pi)
    square = angle * angle
    cosine = 1.0 + square * (-1 / 2 + square * (1 / 24 + square * (-1 / 720 + square * (1 / 40320))))
    sine = 1.0 + square * (-1 / 6 + square * (1 / 120 + square * (-1 / 5040 + square * (1 / 362880))))
    sine = angle * sine
    quarter = quarter.astype(jnp.int32)
    crossed = (quarter & 1) != 0
    first = jnp.where(crossed, sine, cosine)
    second = jnp.where(crossed, cosine, sine)
    first = jnp.where(((quarter + 1) & 2) != 0, -first, first)
    second = jnp.where((quarter & 2) != 0, -second, second)
    return first, second


def write_lists(group, blocks, whole_ref, turn_ref):
    count = len(blocks)
    notes = [
        jnp.concatenate([ref[place], ref[place + 1]], axis=1).astype(jnp.float32) for _, _, (ref, place) in blocks
    ]
    homes = jnp.concatenate([jnp.full((1, PIX), at * 4.0 * BLOCKS, jnp.float32) for at in range(count)], axis=0)
    rows, chosen, cosines, sines = [], [], [], []
    for slot in range(2):
        pulse = jnp.concatenate([note[slot : slot + 1] for note in notes], axis=0)
        start = jnp.concatenate([note[2 + slot : 3 + slot] for note in notes], axis=0)
        errors = [
            jnp.concatenate([note[at : at + 1] + note[at + 1 : at + 2] + note[at + 2 : at + 3] for note in notes], axis=0)
            for at in (4, 7)
        ]
        errors = jnp.where(pulse < 0.5, errors[0], errors[1]) * (0.5 / math.pi)
        cosine, sine = cos_sin(kappa_turns(128.0 * start) - errors)
        filled = pulse < 1.5
        pair = jnp.floor(0.5 * start)
        rows.append((2.0 * (start - 2.0 * pair) + jnp.minimum(pulse, 1.0)) * BLOCKS + pair + homes)
        chosen.append(pulse)
        cosines.append(jnp.where(filled, cosine, 0.0))
        sines.append(jnp.where(filled, sine, 0.0))
    shift = (TILES - group * PLANE) % TILES
    for parts, ref in ((rows + chosen, whole_ref), (cosines + sines, turn_ref)):
        parts = jnp.concatenate(parts + [jnp.zeros((128 - 4 * count, TILES), jnp.float32)], axis=0)
        parts = pltpu.roll(parts, shift, 1)[:, :128]
        ref[...] = parts.T[:PLANE].astype(ref.dtype)


def phase_kernel(group_ref, rate_ref, known_ref, bins_ref, phase_ref, facts_ref):
    facts_ref[...] = jnp.swapaxes(known_ref[...].astype(jnp.float32), 0, 1)
    cross = facts_ref[8] + facts_ref[9] + facts_ref[10]
    for dev in range(GROUPS):
        bins = facts_ref[group_ref[dev]] + 256.0
        phase_ref[dev, 0], phase_ref[dev, 1] = cos_sin(kappa_turns(bins) + rate_ref[dev] * cross)
        bins_ref[dev] = bins.astype(jnp.int32)


def phases(groups, rates, known):
    return pl.pallas_call(
        phase_kernel,
        out_shape=(
            jax.ShapeDtypeStruct((GROUPS, PLANE, PIX), jnp.int32),
            jax.ShapeDtypeStruct((GROUPS, 2, PLANE, PIX), jnp.float32),
        ),
        in_specs=[SMEM, SMEM, VMEM],
        out_specs=(VMEM, VMEM),
        scratch_shapes=[pltpu.VMEM((16, PLANE, PIX), jnp.float32)],
        compiler_params=PARAMS,
        cost_estimate=pl.CostEstimate(flops=1_200_000_000, bytes_accessed=1_000_000, transcendentals=0),
        name="phases",
    )(groups, rates, known)


def pick_lanes(rows, lanes):
    dims = lax.GatherDimensionNumbers(
        offset_dims=(),
        collapsed_slice_dims=(1,),
        start_index_map=(1,),
        operand_batching_dims=(0,),
        start_indices_batching_dims=(0,),
    )
    return lax.gather(rows, lanes[..., None], dims, slice_sizes=(1, 1), mode="promise_in_bounds")


def image_kernel(first, count, parts, last, group_ref, bins_ref, phase_ref, *refs):
    blocks = [pieces(refs[at * parts : (at + 1) * parts]) for at in range(count)]
    refs = refs[count * parts :]
    if first:
        before_ref, refs = refs[0], refs[1:]
    part_ref, kept_ref, lists_ref, comp_ref, turns_ref, whole_ref, turn_ref, sems, *rest = refs
    sum_ref = rest[0] if last else part_ref
    write_lists(group_ref[0], blocks, lists_ref, turns_ref)
    copies = [
        pltpu.make_async_copy(lists_ref, whole_ref, sems.at[0]),
        pltpu.make_async_copy(turns_ref, turn_ref, sems.at[1]),
    ]
    for copy in copies:
        copy.start()
    write_pairs(blocks, comp_ref)
    for copy in copies:
        copy.wait()
    sign = row_sign((ROWS, 128), 0)

    def step(tile, carry):
        total = [before_ref[tile, :, :128], before_ref[tile, :, 128:]] if first else [None, None]
        for at in range(count):
            dev = first + at
            bins = bins_ref[dev, pl.ds(tile, 1), :]
            cos_row = phase_ref[dev, 0, pl.ds(tile, 1), :]
            sin_row = phase_ref[dev, 1, pl.ds(tile, 1), :]
            sources = []
            for slot in range(2):
                base = whole_ref[tile, slot * count + at]
                sources.append((comp_ref[base], comp_ref[base + 1]))
            cos_rot = [turn_ref[tile, slot * count + at] for slot in range(2)]
            sin_rot = [turn_ref[tile, (2 + slot) * count + at] * sign for slot in range(2)]
            for half in range(2):
                lanes = slice(half * 128, (half + 1) * 128)
                where = jnp.broadcast_to(bins[:, lanes], (ROWS, 128))
                lane = where & 127
                odd = (where & 128) != 0
                high = (where & 256) != 0
                lane = jnp.concatenate([lane, lane], axis=0).astype(jnp.int16)
                turned = []
                for slot in range(2):
                    low, top = [pick_lanes(source, lane).astype(jnp.float32) for source in sources[slot]]
                    value = jnp.where(
                        high, jnp.where(odd, top[ROWS:], top[:ROWS]), jnp.where(odd, low[ROWS:], low[:ROWS])
                    )
                    turned.append(cos_rot[slot] * value + sin_rot[slot] * pltpu.roll(value, POLS, 0))
                turned = jnp.concatenate(turned, axis=0).astype(jnp.bfloat16)
                kept_ref[tile, at, :, lanes] = turned
                turned = turned.astype(jnp.float32)
                summed = turned[:ROWS] + turned[ROWS:]
                term = jnp.broadcast_to(cos_row[:, lanes], (ROWS, 128)) * summed + jnp.broadcast_to(
                    sin_row[:, lanes], (ROWS, 128)
                ) * (sign * pltpu.roll(summed, POLS, 0))
                total[half] = term if total[half] is None else total[half] + term
        sum_ref[tile] = jnp.concatenate(total, axis=1)
        return carry

    lax.fori_loop(0, PLANE, step, 0, unroll=16 if last else 8)
    if last:
        part_ref[...] = sum_ref[...].reshape(PLANE * ROWS, PIX).astype(jnp.bfloat16)


def image_parts(first, group, bins, phase, pulses, before=()):
    count, parts = len(pulses), len(pulses[0])
    pulses = [piece for block in pulses for piece in block]
    last = first + count == GROUPS
    part = ((PLANE * ROWS, PIX), jnp.bfloat16) if last else ((PLANE, ROWS, PIX), jnp.float32)
    return pl.pallas_call(
        functools.partial(image_kernel, first, count, parts, last),
        out_shape=(
            jax.ShapeDtypeStruct(*part),
            jax.ShapeDtypeStruct((PLANE, count, 2 * ROWS, PIX), jnp.bfloat16),
            jax.ShapeDtypeStruct((PLANE, 128), jnp.int32),
        ),
        in_specs=[SMEM] + [VMEM] * (2 + len(pulses) + len(before)),
        out_specs=(VMEM, VMEM, VMEM),
        scratch_shapes=[
            pltpu.VMEM((count * 4 * BLOCKS, 2 * ROWS, 128), jnp.bfloat16),
            pltpu.VMEM((PLANE, 128), jnp.float32),
            pltpu.SMEM((PLANE, 128), jnp.int32),
            pltpu.SMEM((PLANE, 128), jnp.float32),
            pltpu.SemaphoreType.DMA((2,)),
        ]
        + ([pltpu.VMEM((PLANE, ROWS, PIX), jnp.float32)] if last else []),
        compiler_params=PARAMS,
        cost_estimate=pl.CostEstimate(flops=100_000_000 * count, bytes_accessed=1_000_000, transcendentals=0),
        name="image",
    )(group, bins, phase, *pulses, *before)


def total_kernel(parts_ref, tile_ref, copies_ref):
    image = IMAGE_SCALE * jnp.sum(parts_ref[...].astype(jnp.float32), axis=0)
    for row in range(ROWS):
        tile_ref[row % POLS, row // POLS, :] = image[row]
    for at in range(PLANE):
        copies_ref[at] = image


def total_image(parts):
    return pl.pallas_call(
        total_kernel,
        out_shape=(
            jax.ShapeDtypeStruct((POLS, 2, PIX), jnp.float32),
            jax.ShapeDtypeStruct((PLANE, ROWS, PIX), jnp.float32),
        ),
        in_specs=[VMEM],
        out_specs=(VMEM, VMEM),
        compiler_params=PARAMS,
        name="total",
    )(parts)


def grad_kernel(group_ref, whole_a, whole_b, image_ref, kept_a, kept_b, phase_ref, out_ref):
    sign = row_sign((ROWS, 128), 0)

    def step(tile, sums):
        sums = list(sums)
        firsts, seconds = [], []
        for half in range(2):
            image = image_ref[tile, :, half * 128 : (half + 1) * 128]
            other = pltpu.roll(image, POLS, 0)
            size = 4.0 * (image * image + other * other)
            firsts.append(size * image)
            seconds.append((size * other) * sign)
        for dev in range(GROUPS):
            cos_row = phase_ref[dev, 0, pl.ds(tile, 1), :]
            sin_row = phase_ref[dev, 1, pl.ds(tile, 1), :]
            weights = []
            for half in range(2):
                lanes = slice(half * 128, (half + 1) * 128)
                weights.append(
                    firsts[half] * jnp.broadcast_to(sin_row[:, lanes], (ROWS, 128))
                    + seconds[half] * jnp.broadcast_to(cos_row[:, lanes], (ROWS, 128))
                )
            whole_ref, kept_ref, at = (whole_a, kept_a, dev) if dev < EARLY else (whole_b, kept_b, dev - EARLY)
            count = EARLY if dev < EARLY else GROUPS - EARLY
            kept = kept_ref[tile, at].astype(jnp.float32)
            for slot in range(2):
                value = kept[slot * ROWS : (slot + 1) * ROWS]
                term = weights[0] * value[:, :128] + weights[1] * value[:, 128:]
                pulse = whole_ref[tile, (2 + slot) * count + at]
                for which in range(2):
                    home = dev * 2 + which
                    sums[home] = sums[home] + jnp.where(pulse == which, 1.0, 0.0) * term
        return tuple(sums)

    zero = jnp.zeros((ROWS, 128), jnp.float32)
    sums = lax.fori_loop(0, PLANE, step, (zero,) * (2 * GROUPS), unroll=4)
    rows = jnp.concatenate([jnp.sum(part, axis=0, keepdims=True) for part in sums], axis=0)
    totals = jnp.sum(rows, axis=1, keepdims=True) * GRAD_SCALE
    lane = lax.broadcasted_iota(jnp.int32, (1, 128), 1)
    for dev in range(GROUPS):
        out_ref[group_ref[dev]] = jnp.where(lane == 0, totals[2 * dev : 2 * dev + 1], totals[2 * dev + 1 : 2 * dev + 2])


def grad_parts(groups, wholes, image, kepts, phase):
    return pl.pallas_call(
        grad_kernel,
        out_shape=jax.ShapeDtypeStruct((GROUPS, 1, 128), jnp.float32),
        in_specs=[SMEM, SMEM, SMEM] + [VMEM] * 4,
        out_specs=VMEM,
        compiler_params=PARAMS,
        name="grad",
    )(groups, *wholes, image, *kepts, phase)


def body(raw_pulses, chirp_taps, phase_error, illumination, swath_start, range_bins, cross_range):
    core = lax.axis_index("core")
    at_y = lax.axis_index("y")
    at_plane = lax.axis_index(("x", "z"))
    groups = jnp.stack([2 * ((at_y + 4 - back) % 4) + (core + other) % 2 for back, other in BLOCK_ORDER])
    rates = (2 * (groups * PLANE + at_plane) + 1 - TILES).astype(jnp.float32) / (2 * TILES)

    raw = raw_pulses.reshape(2, POLS, 2, BLOCKS, BLOCK).transpose(0, 3, 2, 1, 4)
    own, known = compress(
        raw.reshape(2 * BLOCKS * ROWS, BLOCK),
        jnp.pad(chirp_taps, ((0, 0), (0, SPAN - TAPS))),
        phase_error,
        illumination[0].T,
        swath_start[0].T,
        range_bins[0],
        cross_range,
    )
    def back_by(x, steps):
        return lax.ppermute(x, "y", [(at, (at + steps) % 4) for at in range(4)])

    def pair(*block):
        return [block, tuple(lax.ppermute(x, "core", [(0, 1), (1, 0)]) for x in block)]

    near, far = back_by(own, 1), back_by(own, 3)
    across = lax.ppermute(
        onward(core.reshape(1), near, far),
        ("y", "core"),
        [(2 * at, 2 * ((at + 1) % 4)) for at in range(4)] + [(2 * at + 1, 2 * ((at + 3) % 4) + 1) for at in range(4)],
    )
    known = lax.all_to_all(known, ("x", "z"), 0, 0, tiled=True)
    bins, phase = phases(groups, rates, known)
    before, kept_a, whole_a = image_parts(0, groups[:1], bins, phase, pair(own) + pair(near) + pair(far))
    across = lax.optimization_barrier((across, before))[0]
    pulses = pair(across)
    pulses[0] = (fetched(across),)
    parts, kept_b, whole_b = image_parts(EARLY, groups[:1], bins, phase, pulses, (before,))
    parts = lax.all_to_all(parts.reshape(PLANE, ROWS, PIX), ("x", "z"), 0, 0, tiled=True)
    image_tile, copies = total_image(parts)
    images = lax.all_to_all(copies, ("x", "z"), 0, 0, tiled=True)
    grads = grad_parts(groups, (whole_a, whole_b), images, (kept_a, kept_b), phase)
    grads = lax.all_to_all(grads, ("y", "core"), 0, 0, tiled=True)
    return (image_tile[None], jnp.sum(grads[:, 0, :2], axis=0))


def solution(mesh):
    fine = Mesh(mesh.devices.reshape(4, 2, 4, 8), ("y", "core", "x", "z"))
    every = ("y", "core", "x", "z")
    return jax.shard_map(
        body,
        mesh=fine,
        in_specs=(
            P(every, None, None, None),
            P(),
            P(every),
            P(every, None, None),
            P(every, None, None),
            P(every, None, None),
            P(every, None),
        ),
        out_specs=(P(every, None, None, None), P(every)),
        check_vma=False,
    )
```
